256 devices in a mesh: section: 4 (over x), tile: 64 (over z, y, core).
Axes of the slice: x: 4, y: 4, z: 8, core: 2. Of those that a mesh axis runs over, the one named last changes fastest.
Arguments:
- latents: bfloat16 [16, 64, 4, 24, 384], P('section', 'tile'), may hold values from -6 to 6
- frame_counts: int32 [4], replicated, may hold values from 2 to 4, as said below
- norm_gain: float32 [384], replicated, may hold values from 0.1 to 1.9
- conv_weight: bfloat16 [3, 3, 3, 384, 384], replicated, may hold values from -0.0625 to 0.0625
- up_weight: bfloat16 [3, 3, 384, 192], replicated, may hold values from -0.109375 to 0.109375
- pixel_grad: bfloat16 [16, 64, 8, 24, 384], P('section', 'tile'), may hold values from -6 to 6
Outputs:
- decoded: bfloat16 [16, 64, 8, 24, 384], P('section', 'tile')
- latent_grad: float32 [16, 64, 4, 24, 384], P('section', 'tile')
The draws below stay inside these ranges and needn't reach their ends.
Inputs may be any that keep to these rules, and one draw needn't show every extreme that they name: `frame_counts`: every group has at least two frames; some group is full in every draw.
All inputs are finite; a program needn't handle non-finite values.
Results may differ from the reference program's by a relative error of at most 0.0058.
Values may be sent and summed in bfloat16 or wider, within the bound.
No kernel may reach another device: no remote copies, remote signals or barrier semaphores. Data moves between devices by JAX's collectives and lax.ppermute only.
A program may use at most 64 MiB of HBM per device.

```python
import jax
import jax.numpy as jnp
from jax import lax

C = 384
C2 = 192
FMAX = 4
GCOL = 4
BR = 4
BW = 24
GROUPS = 4
FRAMES = 16
N_TILE = 64


def draw_frame_counts(key, part):
    first, second = jax.random.split(key)
    counts = jax.random.randint(first, (GROUPS,), 2, FMAX + 1)
    fullest = jax.random.randint(second, (), 0, GROUPS)
    return jnp.where(jnp.arange(GROUPS) == fullest, FMAX, counts).astype(jnp.int32)


def block_levels(rng, extent, cuts, low, top_value):
    def one(axis_at, shards_of):
        heights = jax.random.uniform(jax.random.fold_in(jax.random.fold_in(rng, 6), axis_at), (shards_of,), jnp.float32, low / len(cuts), top_value / len(cuts))
        return jnp.repeat(jnp.exp(heights), extent[axis_at] // shards_of).reshape((-1,) + (1,) * (len(extent) - axis_at - 1))

    factor_of = one(*cuts[0])
    for cut in cuts[1:]:
        factor_of = factor_of * one(*cut)
    return factor_of


def centred(rng, shape, scale, limit, pieces=(), held_as=jnp.bfloat16):
    result = jax.random.normal(rng, shape, jnp.float32) * scale
    if len(pieces) > 0:
        result = block_levels(rng, shape, pieces, -0.22, 0.18) * result
    return jnp.clip(result, min=-limit, max=limit).astype(held_as)


def setup_inputs(seed: int = 0) -> dict:
    seeds = jax.random.split(jax.random.key(seed), 7)
    return {
        "latents": centred(seeds[0], (FRAMES, N_TILE, BR, BW, C), 1.0, 6.0, ((0, 4), (1, 64))),
        "frame_counts": draw_frame_counts(jax.random.fold_in(seeds[6], 71), 0),
        "norm_gain": jnp.clip(1.0 + 0.18 * jax.random.normal(seeds[2], (C,), jnp.float32), 0.1, 1.9),
        "conv_weight": centred(seeds[3], (3, 3, 3, C, C), (27 * C) ** -0.5, 0.0625),
        "up_weight": centred(seeds[4], (3, 3, C, C2), (9 * C) ** -0.5, 0.109375),
        "pixel_grad": centred(seeds[5], (FRAMES, N_TILE, 2 * BR, BW, 2 * C2), 1.0, 6.0, ((0, 4), (1, 64))),
    }


EPS = 1e-06

def activate(values, gain):
    floats = values.astype(jnp.float32)
    scale = lax.rsqrt(lax.optimization_barrier(jnp.mean(floats * floats, axis=-1, keepdims=True)) + EPS)
    normed = floats * scale * gain
    return normed * jax.nn.sigmoid(normed)

def to_image(blocks):
    placed = jnp.roll(blocks, GCOL + 1, axis=1)
    frames, count, rows, cols, chans = placed.shape
    rowblocks = count // GCOL
    grid = placed.reshape(frames, rowblocks, GCOL, rows, cols, chans)
    return jnp.transpose(grid, (0, 1, 3, 2, 4, 5)).reshape(frames, rowblocks * rows, GCOL * cols, chans)

def from_image(image, rows, cols):
    frames, height, width, chans = image.shape
    rowblocks = height // rows
    grid = image.reshape(frames, rowblocks, rows, GCOL, cols, chans)
    placed = jnp.transpose(grid, (0, 1, 3, 2, 4, 5)).reshape(frames, rowblocks * GCOL, rows, cols, chans)
    return jnp.roll(placed, -(GCOL + 1), axis=1)

def conv_three(extended, weight):
    return lax.conv_general_dilated(extended[None], weight, (1, 1, 1), ((0, 0), (1, 1), (1, 1)), dimension_numbers=('NDHWC', 'DHWIO', 'NDHWC'), preferred_element_type=jnp.float32)[0]

def conv_plane(image, weight):
    return lax.conv_general_dilated(image, weight, (1, 1), ((1, 1), (1, 1)), dimension_numbers=('NHWC', 'HWIO', 'NHWC'), preferred_element_type=jnp.float32)

def place(grad_hidden, future, length):
    frames = grad_hidden.shape[0]
    padded = jnp.concatenate([grad_hidden, jnp.zeros((2,) + grad_hidden.shape[1:], grad_hidden.dtype)], 0)
    slots = jnp.arange(frames + 2, dtype=jnp.int32)[:, None, None, None]
    return jnp.where(slots == length, future[0][None], jnp.where(slots == length + 1, future[1][None], padded))

def reference(latents, frame_counts, norm_gain, conv_weight, up_weight, pixel_grad):
    groups = frame_counts.shape[0]
    frames = latents.shape[0] // groups
    rows, cols = (latents.shape[2], latents.shape[3])
    image = to_image(latents)
    grad_image = to_image(pixel_grad)
    height, width, chans = (image.shape[1], image.shape[2], image.shape[3])
    acts = activate(image, norm_gain).astype(jnp.bfloat16)
    flipped_one = jnp.transpose(jnp.flip(conv_weight, (0, 1, 2)), (0, 1, 2, 4, 3))
    flipped_two = jnp.transpose(jnp.flip(up_weight, (0, 1)), (0, 1, 3, 2))
    position = jnp.arange(frames, dtype=jnp.int32)
    cache = jnp.zeros((2, height, width, chans), jnp.bfloat16)
    decoded_parts = []
    hidden_grads = []
    masks = []
    for group in range(groups):
        length = frame_counts[group]
        mask = (position < length)[:, None, None, None]
        masks.append(mask)
        own = acts[group * frames:(group + 1) * frames]
        extended = jnp.concatenate([cache, own], 0)
        hidden = conv_three(extended, conv_weight).astype(jnp.bfloat16)
        upsampled = jnp.repeat(jnp.repeat(hidden, 2, axis=1), 2, axis=2)
        output = conv_plane(upsampled, up_weight).reshape(frames, 2 * height, width, -1)
        decoded_parts.append(jnp.where(mask, output, 0.0).astype(jnp.bfloat16))
        cache = lax.dynamic_slice_in_dim(own, (length - 2).astype(jnp.int32), 2, 0)
        grad_group = grad_image[group * frames:(group + 1) * frames]
        grad_out = jnp.where(mask, grad_group, jnp.zeros_like(grad_group))
        grad_plane = grad_out.reshape(frames, 2 * height, 2 * width, -1)
        grad_up = conv_plane(grad_plane, flipped_two)
        grad_hidden = grad_up.reshape(frames, height, 2, width, 2, chans).sum(axis=(2, 4)).astype(jnp.bfloat16)
        hidden_grads.append(grad_hidden)
    act_grads = []
    for group in range(groups):
        if group + 1 < groups:
            future = hidden_grads[group + 1][:2]
        else:
            future = jnp.zeros((2, height, width, chans), jnp.bfloat16)
        grad_ext = place(hidden_grads[group], future, frame_counts[group])
        act_grads.append(conv_three(grad_ext, flipped_one))
    grad_acts = jnp.concatenate(act_grads, 0)
    _, pull = jax.vjp(lambda values: activate(values, norm_gain), image.astype(jnp.float32))
    latent_grad = pull(grad_acts)[0]
    frame_mask = jnp.concatenate(masks, 0)
    latent_grad = jnp.where(frame_mask, latent_grad, 0.0).astype(jnp.float32)
    decoded = jnp.concatenate(decoded_parts, 0)
    return (from_image(decoded, 2 * rows, cols), from_image(latent_grad, rows, cols))
```

```python
import functools

import jax
import jax.numpy as jnp
from jax import lax
from jax.experimental import pallas as pl
from jax.experimental.pallas import tpu as pltpu
from jax.sharding import PartitionSpec as P

GCOL = 4
EPS = 1e-06
F, BR, BW, C, CP = 4, 4, 24, 384, 32
BF, F32 = jnp.bfloat16, jnp.float32
NT = (((1,), (1,)), ((), ()))
VM = pl.BlockSpec(memory_space=pltpu.VMEM)
SM = pl.BlockSpec(memory_space=pltpu.SMEM)
ANY = pl.BlockSpec(memory_space=pl.ANY)


def place_of(axis_sizes):
    sections, tiles = axis_sizes
    at = lax.rem(lax.axis_index("tile") + GCOL + 1, tiles)
    row, col = lax.div(at, GCOL), lax.rem(at, GCOL)
    section = lax.axis_index("section")
    return dict(
        section=section,
        up=row > 0,
        down=row < tiles // GCOL - 1,
        left=col > 0,
        right=col < GCOL - 1,
        before=section > 0,
        after=section < sections - 1,
    )


def column_mask(where, width, valid):
    column = lax.broadcasted_iota(jnp.int32, (1, CP, C), 1)
    own = column < BW
    right = (column >= BW) & (column < BW + valid) & where["right"]
    left = (column >= CP - valid) & where["left"]
    return own | right | left


def activate(values, gain):
    scale = lax.rsqrt(jnp.mean(values * values, axis=-1, keepdims=True) + EPS)
    normed = values * scale * gain
    return normed * jax.nn.sigmoid(normed)


def shifted(x, by):
    return pltpu.roll(x, (-by) % CP, axis=x.ndim - 2)


def acts_kernel(sizes, lat, halo, gain, out):
    where = place_of(sizes)
    mask = column_mask(where, C, 2)
    g = gain[...].reshape(1, 1, C)
    for f in range(F):
        whole = jnp.concatenate(
            [lat[f].astype(F32), halo[f, 0:BR].astype(F32)], axis=1
        )
        out[f] = jnp.where(mask, activate(whole, g), 0.0).astype(BF)


def grad_hidden_kernel(sizes, counts, pg, halo, upw, out, parts, acc):
    where = place_of(sizes)
    length = counts[where["section"]]
    mask = column_mask(where, C, 2)
    low = lax.broadcasted_iota(jnp.int32, (1, CP, C), 2) < C // 2
    for f in range(F):
        for r in range(0, 2 * BR, 2):
            whole = jnp.concatenate(
                [pg[f, r : r + 2].astype(F32), halo[f, BR + r : BR + r + 2].astype(F32)], axis=1
            )
            whole = jnp.where(mask & (f < length), whole, 0.0)
            mix = jnp.where(low, shifted(whole, 1), shifted(whole, -1))
            for k in range(2):
                rows = slice((r // 2) * CP, (r // 2 + 1) * CP)
                parts[k, f, rows, 0:C] = whole[k].astype(BF)
                parts[k, f, rows, C : 2 * C] = mix[k].astype(BF)
    even = parts[0].reshape(F * BR * CP, 2 * C)
    odd = parts[1].reshape(F * BR * CP, 2 * C)

    def term(x, w):
        return lax.dot_general(x, upw[w], NT, preferred_element_type=F32).reshape(F, BR * CP, C)

    acc[:, CP : 5 * CP] = term(even, 0) + term(odd, 2)
    acc[:, 0:CP] = jnp.zeros((F, CP, C), F32)
    acc[:, 5 * CP : 6 * CP] = jnp.zeros((F, CP, C), F32)
    acc[:, 0 : 4 * CP] += term(even, 1)
    acc[:, 2 * CP : 6 * CP] += term(odd, 3)
    inner = column_mask(where, C, 1)
    for f in range(F):
        value = acc[f].reshape(6, CP, C)
        row = lax.broadcasted_iota(jnp.int32, (6, CP, C), 0)
        keep = inner & ((row > 0) | where["up"]) & ((row < 5) | where["down"])
        out[f] = jnp.where(keep, value, 0.0).astype(BF)


def back_kernel(gh, weight, acc_out, early_out, wt, cells, acc, sems):
    copies = {}
    for dt in (2, 1, 0):
        for dr in range(3):
            for dc in range(3):
                copy = pltpu.make_async_copy(
                    weight.at[dt, dr, dc],
                    wt.at[dt, dr * C : (dr + 1) * C, dc * C : (dc + 1) * C],
                    sems.at[dt * 9 + dr * 3 + dc],
                )
                copy.start()
                copies[dt, dr, dc] = copy
    for f in range(F):
        value = gh[f].astype(F32)
        for dc in range(3):
            moved = value if dc == 1 else shifted(value, 1 - dc)
            cells[f, :, dc * C : (dc + 1) * C] = moved[:, 0:BW].reshape(6 * BW, C).astype(BF)
    acc[...] = jnp.zeros(acc.shape, F32)
    left = cells[...].reshape(F * 6 * BW, 3 * C)
    for dt in (2, 1, 0):
        for dr in range(3):
            for dc in range(3):
                copies[dt, dr, dc].wait()
        product = lax.dot_general(left, wt[dt], NT, preferred_element_type=F32)
        for f in range(F):
            for dr in range(3):
                acc[f + dt, dr * BW : (dr + 6) * BW] += product[
                    f * 6 * BW : (f + 1) * 6 * BW, dr * C : (dr + 1) * C
                ]
    early_out[...] = acc[0:2].astype(BF)
    acc_out[...] = acc[2:6]


def edge_frames_kernel(sizes, counts, own, above, below, out):
    where = place_of(sizes)
    length = counts[where["section"]]
    for k in range(2):
        f = length - 2 + k
        out[k, 0:2] = jnp.where(where["up"], above[f], jnp.zeros((2, CP, C), BF))
        out[k, 2:6] = own[f]
        out[k, 6:8] = jnp.where(where["down"], below[f], jnp.zeros((2, CP, C), BF))


def side_by_side(x, rows, cells, f):
    for dc in range(3):
        moved = x if dc == 1 else shifted(x, dc - 1)
        count = x.shape[0] * CP
        cells[f, rows * CP : rows * CP + count, dc * C : (dc + 1) * C] = moved.reshape(
            count, C
        ).astype(BF)


def forward_kernel(sizes, own, above, below, weight, acc_out, wt, cells, sems):
    copies = {}
    for dt in (2, 1, 0):
        for dr in range(3):
            copy = pltpu.make_async_copy(weight.at[dt, dr], wt.at[dt * 3 + dr], sems.at[dt * 3 + dr])
            copy.start()
            copies[dt, dr] = copy
    where = place_of(sizes)
    for f in range(F):
        side_by_side(jnp.where(where["up"], above[f].astype(F32), 0.0), 0, cells, f)
        side_by_side(own[f].astype(F32), 2, cells, f)
        side_by_side(jnp.where(where["down"], below[f].astype(F32), 0.0), 6, cells, f)
    for dt in (2, 1, 0):
        count = F - (2 - dt)
        total = None
        for dr in range(3):
            copies[dt, dr].wait()
            left = cells[0:count, dr * CP : (dr + 6) * CP].reshape(count * 6 * CP, 3 * C)
            term = jnp.dot(left, wt[dt * 3 + dr], preferred_element_type=F32)
            total = term if total is None else total + term
        total = total.reshape(count, 6 * CP, C)
        if dt == 2:
            acc_out[...] = total
        else:
            acc_out[2 - dt : F] += total


def decode_kernel(sizes, counts, part, prior, weight, upw, out, wt, cells, pairs, sems):
    copies = {}
    for dt in (0, 1):
        for dr in range(3):
            copy = pltpu.make_async_copy(weight.at[dt, dr], wt.at[dt * 3 + dr], sems.at[dt * 3 + dr])
            copy.start()
            copies[dt, dr] = copy
    where = place_of(sizes)
    length = counts[where["section"]]
    for k in range(2):
        side_by_side(jnp.where(where["before"], prior[k].astype(F32), 0.0), 0, cells, k)

    def term(first, count, dt):
        total = None
        for dr in range(3):
            left = cells[first : first + count, dr * CP : (dr + 6) * CP].reshape(count * 6 * CP, 3 * C)
            value = jnp.dot(left, wt[dt * 3 + dr], preferred_element_type=F32)
            total = value if total is None else total + value
        return total.reshape(count, 6 * CP, C)

    for dr in range(3):
        copies[0, dr].wait()
    early = part[0:2] + term(0, 2, 0)
    for dr in range(3):
        copies[1, dr].wait()
    late = term(1, 1, 1)
    inner = column_mask(where, C, 1)
    row = lax.broadcasted_iota(jnp.int32, (6, CP, C), 0)
    keep = inner & ((row > 0) | where["up"]) & ((row < 5) | where["down"])
    for f in range(F):
        value = part[f] if f >= 2 else early[f]
        if f == 0:
            value = value + late[0]
        hidden = jnp.where(keep, value.reshape(6, CP, C), 0.0).reshape(6 * CP, C).astype(BF)
        pairs[0, f, :, 0:C] = hidden[CP : 5 * CP]
        pairs[0, f, :, C : 2 * C] = hidden[0 : 4 * CP]
        pairs[1, f, :, 0:C] = hidden[CP : 5 * CP]
        pairs[1, f, :, C : 2 * C] = hidden[2 * CP : 6 * CP]
    low = lax.broadcasted_iota(jnp.int32, (1, CP, C), 2) < C // 2
    for k in range(2):
        rows = jnp.dot(
            pairs[k].reshape(F * 4 * CP, 2 * C),
            upw[2 * k : 2 * k + 2].reshape(2 * C, 2 * C),
            preferred_element_type=F32,
        )
        for f in range(F):
            whole = rows[f * 4 * CP : (f + 1) * 4 * CP].reshape(4, CP, 2 * C)
            side = whole[:, :, C : 2 * C]
            mix = jnp.where(low, shifted(side, -1), shifted(side, 1))
            value = jnp.where(f < length, whole[:, :, 0:C] + mix, 0.0)[:, 0:BW].astype(BF)
            for r in range(BR):
                out[f, 2 * r + k] = value[r]


def later_group_kernel(sizes, counts, acc, later, top, bottom, own, total):
    where = place_of(sizes)
    length = counts[where["section"]]
    total[...] = acc[...]
    for k in range(2):
        f = length - 2 + k
        total[f] += jnp.where(where["after"], later[k].astype(F32), 0.0)
    top[...] = total[:, 0 : 2 * BW].astype(BF)
    bottom[...] = total[:, 6 * BW : 8 * BW].astype(BF)
    own[...] = total[:, 2 * BW : 6 * BW]


def latent_grad_kernel(sizes, counts, lat, gain, own, above, below, out):
    where = place_of(sizes)
    length = counts[where["section"]]
    g = gain[...].reshape(1, 1, C)
    for f in range(F):
        x = lat[f].astype(F32)
        upper = own[f, 0 : 2 * BW] + jnp.where(where["up"], above[f].astype(F32), 0.0)
        lower = own[f, 2 * BW : 4 * BW] + jnp.where(where["down"], below[f].astype(F32), 0.0)
        grad = jnp.concatenate([upper, lower], 0).reshape(BR, BW, C)
        scale = lax.rsqrt(jnp.mean(x * x, axis=-1, keepdims=True) + EPS)
        unit = x * scale
        v = unit * g
        s = jax.nn.sigmoid(v)
        t = grad * (s + v * s * (1.0 - s)) * g
        slope = jnp.mean(t * unit, axis=-1, keepdims=True)
        out[f] = jnp.where(f < length, scale * (t - unit * slope), 0.0)


def call(kernel, outs, ins, scratch=(), flops=0, limit=40):
    return pl.pallas_call(
        kernel,
        out_shape=outs,
        in_specs=ins,
        out_specs=jax.tree.map(lambda _: VM, outs),
        scratch_shapes=list(scratch),
        compiler_params=pltpu.CompilerParams(vmem_limit_bytes=limit * 2**20),
        cost_estimate=pl.CostEstimate(flops=flops, bytes_accessed=1000000, transcendentals=0),
    )


def up_taps(up_weight):
    u = up_weight.astype(F32)
    rows = [u[1] + u[2], u[0], u[0] + u[1], u[2]]
    taps = [
        jnp.concatenate([r[1] + r[2], r[0] + r[1], r[0], r[2]], axis=-1).astype(BF) for r in rows
    ]
    return jnp.stack(taps, 0)


def ring(value, axis, steps):
    count = lax.axis_size(axis)
    return lax.ppermute(value, axis, [(i, (i + steps) % count) for i in range(count)])


def per_device(latents, counts, norm_gain, conv_weight, up_weight, pixel_grad):
    sizes = (lax.axis_size("section"), lax.axis_size("tile"))
    lat, pg = latents[:, 0], pixel_grad[:, 0]
    gain = norm_gain.reshape(1, C)
    sd = jax.ShapeDtypeStruct
    kern = lambda k: functools.partial(k, sizes)
    wide = conv_weight.reshape(3, 3, 3 * C, C)

    def strip(a, b):
        return jnp.concatenate([lat[:, :, a:b], pg[:, :, a:b]], 1)

    from_left = ring(strip(BW - 2, BW), "tile", 1)
    from_right = ring(strip(0, 2), "tile", -1)
    upw = up_taps(up_weight)
    halo = jnp.concatenate(
        [from_right, jnp.zeros((F, 3 * BR, 4, C), BF), from_left], 2
    )
    own = call(kern(acts_kernel), sd((F, BR, CP, C), BF), [VM, VM, VM])(lat, halo, gain)
    above = ring(own[:, 2:4], "tile", GCOL)
    below = ring(own[:, 0:2], "tile", -GCOL)
    gh = call(
        kern(grad_hidden_kernel),
        sd((F, 6, CP, C), BF),
        [SM, VM, VM, VM],
        [pltpu.VMEM((2, F, BR * CP, 2 * C), BF), pltpu.VMEM((F, 6 * CP, C), F32)],
        flops=3 * 10**9,
    )(counts, pg, halo, upw)
    acc, early = call(
        back_kernel,
        (sd((F, 8 * BW, C), F32), sd((2, 8 * BW, C), BF)),
        [VM, ANY],
        [
            pltpu.VMEM((3, 3 * C, 3 * C), BF),
            pltpu.VMEM((F, 6 * BW, 3 * C), BF),
            pltpu.VMEM((F + 2, 8 * BW, C), F32),
            pltpu.SemaphoreType.DMA((27,)),
        ],
        flops=6 * 10**9,
    )(gh, conv_weight)
    edge = call(kern(edge_frames_kernel), sd((2, 8, CP, C), BF), [SM, VM, VM, VM])(
        counts, own, above, below
    )
    prior = ring(edge, "section", 1)
    later = ring(early, "section", -1)
    part = call(
        kern(forward_kernel),
        sd((F, 6 * CP, C), F32),
        [VM, VM, VM, ANY],
        [
            pltpu.VMEM((9, 3 * C, C), BF),
            pltpu.VMEM((F, 8 * CP, 3 * C), BF),
            pltpu.SemaphoreType.DMA((9,)),
        ],
        flops=6 * 10**9,
    )(own, above, below, wide)
    top, bottom, mine = call(
        kern(later_group_kernel),
        (sd((F, 2 * BW, C), BF), sd((F, 2 * BW, C), BF), sd((F, 4 * BW, C), F32)),
        [SM, VM, VM],
        [pltpu.VMEM((F, 8 * BW, C), F32)],
    )(counts, acc, later)
    from_above = ring(bottom, "tile", GCOL)
    from_below = ring(top, "tile", -GCOL)
    decoded = call(
        kern(decode_kernel),
        sd((F, 2 * BR, BW, C), BF),
        [SM, VM, VM, ANY, VM],
        [
            pltpu.VMEM((6, 3 * C, C), BF),
            pltpu.VMEM((2, 8 * CP, 3 * C), BF),
            pltpu.VMEM((2, F, 4 * CP, 2 * C), BF),
            pltpu.SemaphoreType.DMA((6,)),
        ],
        flops=4 * 10**9,
    )(counts, part, prior, wide, upw)
    grad = call(
        kern(latent_grad_kernel), sd((F, BR, BW, C), F32), [SM, VM, VM, VM, VM, VM]
    )(counts, lat, gain, mine, from_above, from_below)
    return (decoded[:, None], grad[:, None])


def solution(mesh):
    blocks = P("section", "tile", None, None, None)
    return jax.shard_map(
        per_device,
        mesh=mesh,
        in_specs=(blocks, P(), P(), P(), P(), blocks),
        out_specs=(blocks, blocks),
        check_vma=False,
    )
```

```python
import functools

import jax
import jax.numpy as jnp
from jax import lax
from jax.experimental import pallas as pl
from jax.experimental.pallas import tpu as pltpu
from jax.sharding import PartitionSpec as P

GCOL = 4
EPS = 1e-06
F, BR, BW, C, CP = 4, 4, 24, 384, 32
BF, F32 = jnp.bfloat16, jnp.float32
NT = (((1,), (1,)), ((), ()))
VM = pl.BlockSpec(memory_space=pltpu.VMEM)
SM = pl.BlockSpec(memory_space=pltpu.SMEM)
ANY = pl.BlockSpec(memory_space=pl.ANY)


def place_of(axis_sizes):
    sections, tiles = axis_sizes
    at = lax.rem(lax.axis_index("tile") + GCOL + 1, tiles)
    row, col = lax.div(at, GCOL), lax.rem(at, GCOL)
    section = lax.axis_index("section")
    return dict(
        section=section,
        up=row > 0,
        down=row < tiles // GCOL - 1,
        left=col > 0,
        right=col < GCOL - 1,
        before=section > 0,
        after=section < sections - 1,
    )


def column_mask(where, width, valid):
    column = lax.broadcasted_iota(jnp.int32, (1, CP, C), 1)
    own = column < BW
    right = (column >= BW) & (column < BW + valid) & where["right"]
    left = (column >= CP - valid) & where["left"]
    return own | right | left


def activate(values, gain):
    scale = lax.rsqrt(jnp.mean(values * values, axis=-1, keepdims=True) + EPS)
    normed = values * scale * gain
    return normed * jax.nn.sigmoid(normed)


def shifted(x, by):
    return pltpu.roll(x, (-by) % CP, axis=x.ndim - 2)


def acts_kernel(sizes, lat, halo, gain, out):
    where = place_of(sizes)
    mask = column_mask(where, C, 2)
    g = gain[...].reshape(1, 1, C)
    for f in range(F):
        whole = jnp.concatenate(
            [lat[f].astype(F32), halo[f, 0:BR].astype(F32)], axis=1
        )
        out[f] = jnp.where(mask, activate(whole, g), 0.0).astype(BF)


def up_taps(up, upw):
    rows = (((1, 2), (0,)), ((0, 1), (2,)))
    columns = ((1, 2), (0, 1), (0,), (2,))
    for k in range(2):
        for a in range(2):
            sums = [sum(up[dr, dc].astype(F32) for dr in rows[k][a]) for dc in range(3)]
            for b in range(4):
                total = sum(sums[dc] for dc in columns[b])
                upw[k, b * (C // 2) : (b + 1) * (C // 2), a * C : (a + 1) * C] = total.astype(BF)


def grad_hidden_kernel(sizes, counts, pg, halo, up, own, out, upw, parts, acc):
    where = place_of(sizes)
    up_taps(up, upw)
    length = counts[where["section"]]
    mask = column_mask(where, C, 2)
    low = lax.broadcasted_iota(jnp.int32, (1, CP, C), 2) < C // 2
    for f in range(F):
        for r in range(0, 2 * BR, 2):
            whole = jnp.concatenate(
                [pg[f, r : r + 2].astype(F32), halo[f, BR + r : BR + r + 2].astype(F32)], axis=1
            )
            whole = jnp.where(mask & (f < length), whole, 0.0)
            mix = jnp.where(low, shifted(whole, 1), shifted(whole, -1))
            for k in range(2):
                rows = slice((r // 2) * CP, (r // 2 + 1) * CP)
                parts[k, f, rows, 0:C] = whole[k].astype(BF)
                parts[k, f, rows, C : 2 * C] = mix[k].astype(BF)
    even = parts[0].reshape(F * BR * CP, 2 * C)
    odd = parts[1].reshape(F * BR * CP, 2 * C)

    def term(x, k, a):
        taps = upw[k, :, a * C : (a + 1) * C]
        return jnp.dot(x, taps, preferred_element_type=F32).reshape(F, BR * CP, C)

    acc[:, CP : 5 * CP] = term(even, 0, 0) + term(odd, 1, 0)
    acc[:, 0:CP] = jnp.zeros((F, CP, C), F32)
    acc[:, 5 * CP : 6 * CP] = jnp.zeros((F, CP, C), F32)
    acc[:, 0 : 4 * CP] += term(even, 0, 1)
    acc[:, 2 * CP : 6 * CP] += term(odd, 1, 1)
    inner = column_mask(where, C, 1)
    for f in range(F):
        value = acc[f].reshape(6, CP, C)
        row = lax.broadcasted_iota(jnp.int32, (6, CP, C), 0)
        keep = inner & ((row > 0) | where["up"]) & ((row < 5) | where["down"])
        out[f] = jnp.where(keep, value, 0.0).astype(BF)


def back_kernel(gh, weight, acc_out, early_out, wt, cells, acc, sems):
    copies = {}
    for dt in (2, 1, 0):
        for dr in range(3):
            for dc in range(3):
                copy = pltpu.make_async_copy(
                    weight.at[dt, dr, dc],
                    wt.at[dt, dr * C : (dr + 1) * C, dc * C : (dc + 1) * C],
                    sems.at[dt * 9 + dr * 3 + dc],
                )
                copy.start()
                copies[dt, dr, dc] = copy
    for f in range(F):
        value = gh[f].astype(F32)
        for dc in range(3):
            moved = value if dc == 1 else shifted(value, 1 - dc)
            cells[f, :, dc * C : (dc + 1) * C] = moved[:, 0:BW].reshape(6 * BW, C).astype(BF)
    acc[...] = jnp.zeros(acc.shape, F32)
    left = cells[...].reshape(F * 6 * BW, 3 * C)
    for dt in (2, 1, 0):
        for dr in range(3):
            for dc in range(3):
                copies[dt, dr, dc].wait()
        product = lax.dot_general(left, wt[dt], NT, preferred_element_type=F32)
        for f in range(F):
            for dr in range(3):
                acc[f + dt, dr * BW : (dr + 6) * BW] += product[
                    f * 6 * BW : (f + 1) * 6 * BW, dr * C : (dr + 1) * C
                ]
    early_out[...] = acc[0:2].astype(BF)
    acc_out[...] = acc[2:6]


def edge_frames_kernel(sizes, counts, own, above, below, early, out, early_out):
    early_out[...] = early[...]
    where = place_of(sizes)
    length = counts[where["section"]]
    for k in range(2):
        f = length - 2 + k
        out[k, 0:2] = jnp.where(where["up"], above[f], jnp.zeros((2, CP, C), BF))
        out[k, 2:6] = own[f]
        out[k, 6:8] = jnp.where(where["down"], below[f], jnp.zeros((2, CP, C), BF))


def side_by_side(x, rows, cells, f):
    for dc in range(3):
        moved = x if dc == 1 else shifted(x, dc - 1)
        count = x.shape[0] * CP
        cells[f, rows * CP : rows * CP + count, dc * C : (dc + 1) * C] = moved.reshape(
            count, C
        ).astype(BF)


def forward_kernel(sizes, own, above, below, weight, acc_out, wt, cells, sems):
    copies = {}
    for dt in (2, 1, 0):
        for dr in range(3):
            copy = pltpu.make_async_copy(weight.at[dt, dr], wt.at[dt * 3 + dr], sems.at[dt * 3 + dr])
            copy.start()
            copies[dt, dr] = copy
    where = place_of(sizes)
    for f in range(F):
        side_by_side(jnp.where(where["up"], above[f].astype(F32), 0.0), 0, cells, f)
        side_by_side(own[f].astype(F32), 2, cells, f)
        side_by_side(jnp.where(where["down"], below[f].astype(F32), 0.0), 6, cells, f)
    for dt in (2, 1, 0):
        count = F - (2 - dt)
        total = None
        for dr in range(3):
            copies[dt, dr].wait()
            left = cells[0:count, dr * CP : (dr + 6) * CP].reshape(count * 6 * CP, 3 * C)
            term = jnp.dot(left, wt[dt * 3 + dr], preferred_element_type=F32)
            total = term if total is None else total + term
        total = total.reshape(count, 6 * CP, C)
        if dt == 2:
            acc_out[...] = total
        else:
            acc_out[2 - dt : F] += total


def decode_kernel(sizes, counts, part, prior, weight, upw, out, wt, cells, pairs, sems):
    copies = {}
    for dt in (0, 1):
        for dr in range(3):
            copy = pltpu.make_async_copy(weight.at[dt, dr], wt.at[dt * 3 + dr], sems.at[dt * 3 + dr])
            copy.start()
            copies[dt, dr] = copy
    where = place_of(sizes)
    length = counts[where["section"]]
    for k in range(2):
        side_by_side(jnp.where(where["before"], prior[k].astype(F32), 0.0), 0, cells, k)

    def term(first, count, dt):
        total = None
        for dr in range(3):
            left = cells[first : first + count, dr * CP : (dr + 6) * CP].reshape(count * 6 * CP, 3 * C)
            value = jnp.dot(left, wt[dt * 3 + dr], preferred_element_type=F32)
            total = value if total is None else total + value
        return total.reshape(count, 6 * CP, C)

    for dr in range(3):
        copies[0, dr].wait()
    early = part[0:2] + term(0, 2, 0)
    for dr in range(3):
        copies[1, dr].wait()
    late = term(1, 1, 1)
    inner = column_mask(where, C, 1)
    row = lax.broadcasted_iota(jnp.int32, (6, CP, C), 0)
    keep = inner & ((row > 0) | where["up"]) & ((row < 5) | where["down"])
    for f in range(F):
        value = part[f] if f >= 2 else early[f]
        if f == 0:
            value = value + late[0]
        hidden = jnp.where(keep, value.reshape(6, CP, C), 0.0).reshape(6 * CP, C).astype(BF)
        pairs[0, f, :, 0:C] = hidden[CP : 5 * CP]
        pairs[0, f, :, C : 2 * C] = hidden[0 : 4 * CP]
        pairs[1, f, :, 0:C] = hidden[CP : 5 * CP]
        pairs[1, f, :, C : 2 * C] = hidden[2 * CP : 6 * CP]
    low = lax.broadcasted_iota(jnp.int32, (1, CP, C), 2) < C // 2
    for k in range(2):
        rows = lax.dot_general(
            pairs[k].reshape(F * 4 * CP, 2 * C), upw[k], NT, preferred_element_type=F32
        )
        for f in range(F):
            whole = rows[f * 4 * CP : (f + 1) * 4 * CP].reshape(4, CP, 2 * C)
            side = whole[:, :, C : 2 * C]
            mix = jnp.where(low, shifted(side, -1), shifted(side, 1))
            value = jnp.where(f < length, whole[:, :, 0:C] + mix, 0.0)[:, 0:BW].astype(BF)
            for r in range(BR):
                out[f, 2 * r + k] = value[r]


def later_group_kernel(sizes, counts, acc, later, top, bottom, own, total):
    where = place_of(sizes)
    length = counts[where["section"]]
    total[...] = acc[...]
    for k in range(2):
        f = length - 2 + k
        total[f] += jnp.where(where["after"], later[k].astype(F32), 0.0)
    top[...] = total[:, 0 : 2 * BW].astype(BF)
    bottom[...] = total[:, 6 * BW : 8 * BW].astype(BF)
    own[...] = total[:, 2 * BW : 6 * BW]


def latent_grad_kernel(sizes, counts, lat, gain, own, above, below, out):
    where = place_of(sizes)
    length = counts[where["section"]]
    g = gain[...].reshape(1, 1, C)
    for f in range(F):
        x = lat[f].astype(F32)
        upper = own[f, 0 : 2 * BW] + jnp.where(where["up"], above[f].astype(F32), 0.0)
        lower = own[f, 2 * BW : 4 * BW] + jnp.where(where["down"], below[f].astype(F32), 0.0)
        grad = jnp.concatenate([upper, lower], 0).reshape(BR, BW, C)
        scale = lax.rsqrt(jnp.mean(x * x, axis=-1, keepdims=True) + EPS)
        unit = x * scale
        v = unit * g
        s = jax.nn.sigmoid(v)
        t = grad * (s + v * s * (1.0 - s)) * g
        slope = jnp.mean(t * unit, axis=-1, keepdims=True)
        out[f] = jnp.where(f < length, scale * (t - unit * slope), 0.0)


def call(kernel, outs, ins, scratch=(), flops=0, limit=40):
    return pl.pallas_call(
        kernel,
        out_shape=outs,
        in_specs=ins,
        out_specs=jax.tree.map(lambda _: VM, outs),
        scratch_shapes=list(scratch),
        compiler_params=pltpu.CompilerParams(vmem_limit_bytes=limit * 2**20),
        cost_estimate=pl.CostEstimate(flops=flops, bytes_accessed=1000000, transcendentals=0),
    )


def ring(value, axis, steps):
    count = lax.axis_size(axis)
    return lax.ppermute(value, axis, [(i, (i + steps) % count) for i in range(count)])


def per_device(latents, counts, norm_gain, conv_weight, up_weight, pixel_grad):
    sizes = (lax.axis_size("section"), lax.axis_size("tile"))
    lat, pg = latents[:, 0], pixel_grad[:, 0]
    gain = norm_gain.reshape(1, C)
    sd = jax.ShapeDtypeStruct
    kern = lambda k: functools.partial(k, sizes)
    wide = conv_weight.reshape(3, 3, 3 * C, C)

    def strip(a, b):
        return jnp.concatenate([lat[:, :, a:b], pg[:, :, a:b]], 1)

    from_left = ring(strip(BW - 2, BW), "tile", 1)
    from_right = ring(strip(0, 2), "tile", -1)
    halo = jnp.concatenate(
        [from_right, jnp.zeros((F, 3 * BR, 4, C), BF), from_left], 2
    )
    own = call(kern(acts_kernel), sd((F, BR, CP, C), BF), [VM, VM, VM])(lat, halo, gain)
    above = ring(own[:, 2:4], "tile", GCOL)
    below = ring(own[:, 0:2], "tile", -GCOL)
    gh, upw = call(
        kern(grad_hidden_kernel),
        (sd((F, 6, CP, C), BF), sd((2, 2 * C, 2 * C), BF)),
        [SM, VM, VM, VM, ANY],
        [pltpu.VMEM((2, F, BR * CP, 2 * C), BF), pltpu.VMEM((F, 6 * CP, C), F32)],
        flops=3 * 10**9,
    )(counts, pg, halo, jnp.transpose(up_weight, (0, 1, 3, 2)), own)
    acc, early = call(
        back_kernel,
        (sd((F, 8 * BW, C), F32), sd((2, 8 * BW, C), BF)),
        [VM, ANY],
        [
            pltpu.VMEM((3, 3 * C, 3 * C), BF),
            pltpu.VMEM((F, 6 * BW, 3 * C), BF),
            pltpu.VMEM((F + 2, 8 * BW, C), F32),
            pltpu.SemaphoreType.DMA((27,)),
        ],
        flops=6 * 10**9,
    )(gh, conv_weight)
    edge, early = call(
        kern(edge_frames_kernel),
        (sd((2, 8, CP, C), BF), sd((2, 8 * BW, C), BF)),
        [SM, VM, VM, VM, VM],
    )(counts, own, above, below, early)
    prior = ring(edge, "section", 1)
    later = ring(early, "section", -1)
    part = call(
        kern(forward_kernel),
        sd((F, 6 * CP, C), F32),
        [VM, VM, VM, ANY],
        [
            pltpu.VMEM((9, 3 * C, C), BF),
            pltpu.VMEM((F, 8 * CP, 3 * C), BF),
            pltpu.SemaphoreType.DMA((9,)),
        ],
        flops=6 * 10**9,
    )(own, above, below, wide)
    top, bottom, mine = call(
        kern(later_group_kernel),
        (sd((F, 2 * BW, C), BF), sd((F, 2 * BW, C), BF), sd((F, 4 * BW, C), F32)),
        [SM, VM, VM],
        [pltpu.VMEM((F, 8 * BW, C), F32)],
    )(counts, acc, later)
    from_above = ring(bottom, "tile", GCOL)
    from_below = ring(top, "tile", -GCOL)
    decoded = call(
        kern(decode_kernel),
        sd((F, 2 * BR, BW, C), BF),
        [SM, VM, VM, ANY, VM],
        [
            pltpu.VMEM((6, 3 * C, C), BF),
            pltpu.VMEM((2, 8 * CP, 3 * C), BF),
            pltpu.VMEM((2, F, 4 * CP, 2 * C), BF),
            pltpu.SemaphoreType.DMA((6,)),
        ],
        flops=4 * 10**9,
    )(counts, part, prior, wide, upw)
    grad = call(
        kern(latent_grad_kernel), sd((F, BR, BW, C), F32), [SM, VM, VM, VM, VM, VM]
    )(counts, lat, gain, mine, from_above, from_below)
    return (decoded[:, None], grad[:, None])


def solution(mesh):
    blocks = P("section", "tile", None, None, None)
    return jax.shard_map(
        per_device,
        mesh=mesh,
        in_specs=(blocks, P(), P(), P(), P(), blocks),
        out_specs=(blocks, blocks),
        check_vma=False,
    )
```

```python
import functools

import jax
import jax.numpy as jnp
from jax import lax
from jax.experimental import pallas as pl
from jax.experimental.pallas import tpu as pltpu
from jax.sharding import PartitionSpec as P

GCOL = 4
EPS = 1e-06
F, BR, BW, C, CP = 4, 4, 24, 384, 32
BF, F32 = jnp.bfloat16, jnp.float32
NT = (((1,), (1,)), ((), ()))
VM = pl.BlockSpec(memory_space=pltpu.VMEM)
SM = pl.BlockSpec(memory_space=pltpu.SMEM)
ANY = pl.BlockSpec(memory_space=pl.ANY)


def place_of(axis_sizes):
    sections, tiles = axis_sizes
    at = lax.rem(lax.axis_index("tile") + GCOL + 1, tiles)
    row, col = lax.div(at, GCOL), lax.rem(at, GCOL)
    section = lax.axis_index("section")
    return dict(
        section=section,
        up=row > 0,
        down=row < tiles // GCOL - 1,
        left=col > 0,
        right=col < GCOL - 1,
        before=section > 0,
        after=section < sections - 1,
    )


def column_mask(where, width, valid):
    column = lax.broadcasted_iota(jnp.int32, (1, CP, C), 1)
    own = column < BW
    right = (column >= BW) & (column < BW + valid) & where["right"]
    left = (column >= CP - valid) & where["left"]
    return own | right | left


def activate(values, gain):
    scale = lax.rsqrt(jnp.mean(values * values, axis=-1, keepdims=True) + EPS)
    normed = values * scale * gain
    return normed * jax.nn.sigmoid(normed)


def shifted(x, by):
    return pltpu.roll(x, (-by) % CP, axis=x.ndim - 2)


def acts_kernel(sizes, lat, halo, gain, out):
    where = place_of(sizes)
    mask = column_mask(where, C, 2)
    g = gain[...].reshape(1, 1, C)
    for f in range(F):
        whole = jnp.concatenate(
            [lat[f].astype(F32), halo[f, 0:BR].astype(F32)], axis=1
        )
        out[f] = jnp.where(mask, activate(whole, g), 0.0).astype(BF)


def up_taps(up, upw):
    rows = (((1, 2), (0,)), ((0, 1), (2,)))
    columns = ((1, 2), (0, 1), (0,), (2,))
    for k in range(2):
        for a in range(2):
            sums = [sum(up[dr, dc].astype(F32) for dr in rows[k][a]) for dc in range(3)]
            for b in range(4):
                total = sum(sums[dc] for dc in columns[b])
                upw[k, b * (C // 2) : (b + 1) * (C // 2), a * C : (a + 1) * C] = total.astype(BF)


def grad_hidden_kernel(sizes, counts, pg, halo, up, own, out, upw, parts, acc):
    where = place_of(sizes)
    up_taps(up, upw)
    length = counts[where["section"]]
    mask = column_mask(where, C, 2)
    low = lax.broadcasted_iota(jnp.int32, (1, CP, C), 2) < C // 2
    for f in range(F):
        for r in range(0, 2 * BR, 2):
            whole = jnp.concatenate(
                [pg[f, r : r + 2].astype(F32), halo[f, BR + r : BR + r + 2].astype(F32)], axis=1
            )
            whole = jnp.where(mask & (f < length), whole, 0.0)
            mix = jnp.where(low, shifted(whole, 1), shifted(whole, -1))
            for k in range(2):
                rows = slice((r // 2) * CP, (r // 2 + 1) * CP)
                parts[k, f, rows, 0:C] = whole[k].astype(BF)
                parts[k, f, rows, C : 2 * C] = mix[k].astype(BF)
    even = parts[0].reshape(F * BR * CP, 2 * C)
    odd = parts[1].reshape(F * BR * CP, 2 * C)

    def term(x, k, a):
        taps = upw[k, :, a * C : (a + 1) * C]
        return jnp.dot(x, taps, preferred_element_type=F32).reshape(F, BR * CP, C)

    acc[:, CP : 5 * CP] = term(even, 0, 0) + term(odd, 1, 0)
    acc[:, 0:CP] = jnp.zeros((F, CP, C), F32)
    acc[:, 5 * CP : 6 * CP] = jnp.zeros((F, CP, C), F32)
    acc[:, 0 : 4 * CP] += term(even, 0, 1)
    acc[:, 2 * CP : 6 * CP] += term(odd, 1, 1)
    inner = column_mask(where, C, 1)
    for f in range(F):
        value = acc[f].reshape(6, CP, C)
        row = lax.broadcasted_iota(jnp.int32, (6, CP, C), 0)
        keep = inner & ((row > 0) | where["up"]) & ((row < 5) | where["down"])
        out[f] = jnp.where(keep, value, 0.0).astype(BF)


def back_kernel(gh, weight, acc_out, early_out, wt, cells, acc, sems):
    copies = {}
    for dt in (2, 1, 0):
        for dr in range(3):
            for dc in range(3):
                copy = pltpu.make_async_copy(
                    weight.at[dt, dr, dc],
                    wt.at[dt, dr * C : (dr + 1) * C, dc * C : (dc + 1) * C],
                    sems.at[dt * 9 + dr * 3 + dc],
                )
                copy.start()
                copies[dt, dr, dc] = copy
    for f in range(F):
        value = gh[f].astype(F32)
        for dc in range(3):
            moved = value if dc == 1 else shifted(value, 1 - dc)
            cells[f, :, dc * C : (dc + 1) * C] = moved[:, 0:BW].reshape(6 * BW, C).astype(BF)
    acc[...] = jnp.zeros(acc.shape, F32)
    left = cells[...].reshape(F * 6 * BW, 3 * C)
    for dt in (2, 1, 0):
        for dr in range(3):
            for dc in range(3):
                copies[dt, dr, dc].wait()
        product = lax.dot_general(left, wt[dt], NT, preferred_element_type=F32)
        for f in range(F):
            for dr in range(3):
                acc[f + dt, dr * BW : (dr + 6) * BW] += product[
                    f * 6 * BW : (f + 1) * 6 * BW, dr * C : (dr + 1) * C
                ]
    early_out[...] = acc[0:2].astype(BF)
    acc_out[...] = acc[2:6]


def edge_frames_kernel(sizes, counts, own, above, below, early, out, early_out):
    early_out[...] = early[...]
    where = place_of(sizes)
    length = counts[where["section"]]
    for k in range(2):
        f = length - 2 + k
        out[k, 0:2] = jnp.where(where["up"], above[f], jnp.zeros((2, CP, C), BF))
        out[k, 2:6] = own[f]
        out[k, 6:8] = jnp.where(where["down"], below[f], jnp.zeros((2, CP, C), BF))


def side_by_side(x, rows, cells, f):
    for dc in range(3):
        moved = x if dc == 1 else shifted(x, dc - 1)
        count = x.shape[0] * CP
        cells[f, rows * CP : rows * CP + count, dc * C : (dc + 1) * C] = moved.reshape(
            count, C
        ).astype(BF)


def forward_kernel(sizes, own, above, below, weight, acc_out, cells):
    where = place_of(sizes)
    for f in range(F):
        side_by_side(jnp.where(where["up"], above[f].astype(F32), 0.0), 0, cells, f)
        side_by_side(own[f].astype(F32), 2, cells, f)
        side_by_side(jnp.where(where["down"], below[f].astype(F32), 0.0), 6, cells, f)
    for dt in (2, 1, 0):
        count = F - (2 - dt)
        total = None
        for dr in range(3):
            left = cells[0:count, dr * CP : (dr + 6) * CP].reshape(count * 6 * CP, 3 * C)
            term = jnp.dot(left, weight[dt, dr], preferred_element_type=F32)
            total = term if total is None else total + term
        total = total.reshape(count, 6 * CP, C)
        if dt == 2:
            acc_out[...] = total
        else:
            acc_out[2 - dt : F] += total


def decode_kernel(sizes, counts, part, prior, weight, upw, out, cells, pairs):
    where = place_of(sizes)
    length = counts[where["section"]]
    for k in range(2):
        side_by_side(jnp.where(where["before"], prior[k].astype(F32), 0.0), 0, cells, k)

    def term(first, count, dt):
        total = None
        for dr in range(3):
            left = cells[first : first + count, dr * CP : (dr + 6) * CP].reshape(count * 6 * CP, 3 * C)
            value = jnp.dot(left, weight[dt, dr], preferred_element_type=F32)
            total = value if total is None else total + value
        return total.reshape(count, 6 * CP, C)

    early = part[0:2] + term(0, 2, 0)
    late = term(1, 1, 1)
    inner = column_mask(where, C, 1)
    row = lax.broadcasted_iota(jnp.int32, (6, CP, C), 0)
    keep = inner & ((row > 0) | where["up"]) & ((row < 5) | where["down"])
    for f in range(F):
        value = part[f] if f >= 2 else early[f]
        if f == 0:
            value = value + late[0]
        hidden = jnp.where(keep, value.reshape(6, CP, C), 0.0).reshape(6 * CP, C).astype(BF)
        pairs[0, f, :, 0:C] = hidden[CP : 5 * CP]
        pairs[0, f, :, C : 2 * C] = hidden[0 : 4 * CP]
        pairs[1, f, :, 0:C] = hidden[CP : 5 * CP]
        pairs[1, f, :, C : 2 * C] = hidden[2 * CP : 6 * CP]
    low = lax.broadcasted_iota(jnp.int32, (1, CP, C), 2) < C // 2
    for k in range(2):
        rows = lax.dot_general(
            pairs[k].reshape(F * 4 * CP, 2 * C), upw[k], NT, preferred_element_type=F32
        )
        for f in range(F):
            whole = rows[f * 4 * CP : (f + 1) * 4 * CP].reshape(4, CP, 2 * C)
            side = whole[:, :, C : 2 * C]
            mix = jnp.where(low, shifted(side, -1), shifted(side, 1))
            value = jnp.where(f < length, whole[:, :, 0:C] + mix, 0.0)[:, 0:BW].astype(BF)
            for r in range(BR):
                out[f, 2 * r + k] = value[r]


def later_group_kernel(sizes, counts, acc, later, top, bottom, own, total):
    where = place_of(sizes)
    length = counts[where["section"]]
    total[...] = acc[...]
    for k in range(2):
        f = length - 2 + k
        total[f] += jnp.where(where["after"], later[k].astype(F32), 0.0)
    top[...] = total[:, 0 : 2 * BW].astype(BF)
    bottom[...] = total[:, 6 * BW : 8 * BW].astype(BF)
    own[...] = total[:, 2 * BW : 6 * BW]


def latent_grad_kernel(sizes, counts, lat, gain, own, above, below, out):
    where = place_of(sizes)
    length = counts[where["section"]]
    g = gain[...].reshape(1, 1, C)
    for f in range(F):
        x = lat[f].astype(F32)
        upper = own[f, 0 : 2 * BW] + jnp.where(where["up"], above[f].astype(F32), 0.0)
        lower = own[f, 2 * BW : 4 * BW] + jnp.where(where["down"], below[f].astype(F32), 0.0)
        grad = jnp.concatenate([upper, lower], 0).reshape(BR, BW, C)
        scale = lax.rsqrt(jnp.mean(x * x, axis=-1, keepdims=True) + EPS)
        unit = x * scale
        v = unit * g
        s = jax.nn.sigmoid(v)
        t = grad * (s + v * s * (1.0 - s)) * g
        slope = jnp.mean(t * unit, axis=-1, keepdims=True)
        out[f] = jnp.where(f < length, scale * (t - unit * slope), 0.0)


def call(kernel, outs, ins, scratch=(), flops=0, limit=40):
    return pl.pallas_call(
        kernel,
        out_shape=outs,
        in_specs=ins,
        out_specs=jax.tree.map(lambda _: VM, outs),
        scratch_shapes=list(scratch),
        compiler_params=pltpu.CompilerParams(vmem_limit_bytes=limit * 2**20),
        cost_estimate=pl.CostEstimate(flops=flops, bytes_accessed=1000000, transcendentals=0),
    )


def ring(value, axis, steps):
    count = lax.axis_size(axis)
    return lax.ppermute(value, axis, [(i, (i + steps) % count) for i in range(count)])


def swap(value, tiles, shift):
    places = [((at + GCOL + 1 + shift) ^ 1) - GCOL - 1 - shift for at in range(tiles)]
    return lax.ppermute(value, "tile", [(at, to % tiles) for at, to in enumerate(places)])


def per_device(latents, counts, norm_gain, conv_weight, up_weight, pixel_grad):
    sizes = (lax.axis_size("section"), lax.axis_size("tile"))
    lat, pg = latents[:, 0], pixel_grad[:, 0]
    gain = norm_gain.reshape(1, C)
    sd = jax.ShapeDtypeStruct
    kern = lambda k: functools.partial(k, sizes)
    wide = conv_weight.reshape(3, 3, 3 * C, C)

    tiles = sizes[1]
    even = lax.rem(lax.axis_index("tile") + GCOL + 1, 2) == 0

    def strip(a):
        return jnp.concatenate([lat[:, :, a : a + 2], pg[:, :, a : a + 2]], 1)

    first, last = strip(0), strip(BW - 2)
    one = swap(jnp.where(even, last, first), tiles, 0)
    two = swap(jnp.where(even, first, last), tiles, 1)
    from_left, from_right = jnp.where(even, two, one), jnp.where(even, one, two)
    halo = jnp.concatenate([from_right, jnp.zeros((F, 3 * BR, 4, C), BF), from_left], 2)
    own = call(kern(acts_kernel), sd((F, BR, CP, C), BF), [VM, VM, VM])(lat, halo, gain)
    above = ring(own[:, 2:4], "tile", GCOL)
    below = ring(own[:, 0:2], "tile", -GCOL)
    gh, upw = call(
        kern(grad_hidden_kernel),
        (sd((F, 6, CP, C), BF), sd((2, 2 * C, 2 * C), BF)),
        [SM, VM, VM, VM, ANY],
        [pltpu.VMEM((2, F, BR * CP, 2 * C), BF), pltpu.VMEM((F, 6 * CP, C), F32)],
        flops=3 * 10**9,
    )(counts, pg, halo, jnp.transpose(up_weight, (0, 1, 3, 2)), own)
    acc, early = call(
        back_kernel,
        (sd((F, 8 * BW, C), F32), sd((2, 8 * BW, C), BF)),
        [VM, ANY],
        [
            pltpu.VMEM((3, 3 * C, 3 * C), BF),
            pltpu.VMEM((F, 6 * BW, 3 * C), BF),
            pltpu.VMEM((F + 2, 8 * BW, C), F32),
            pltpu.SemaphoreType.DMA((27,)),
        ],
        flops=6 * 10**9,
    )(gh, conv_weight)
    edge, early = call(
        kern(edge_frames_kernel),
        (sd((2, 8, CP, C), BF), sd((2, 8 * BW, C), BF)),
        [SM, VM, VM, VM, VM],
    )(counts, own, above, below, early)
    prior = ring(edge, "section", 1)
    later = ring(early, "section", -1)
    part = call(
        kern(forward_kernel),
        sd((F, 6 * CP, C), F32),
        [VM, VM, VM, VM],
        [pltpu.VMEM((F, 8 * CP, 3 * C), BF)],
        flops=6 * 10**9,
    )(own, above, below, wide)
    top, bottom, mine = call(
        kern(later_group_kernel),
        (sd((F, 2 * BW, C), BF), sd((F, 2 * BW, C), BF), sd((F, 4 * BW, C), F32)),
        [SM, VM, VM],
        [pltpu.VMEM((F, 8 * BW, C), F32)],
    )(counts, acc, later)
    from_above = ring(bottom, "tile", GCOL)
    from_below = ring(top, "tile", -GCOL)
    decoded = call(
        kern(decode_kernel),
        sd((F, 2 * BR, BW, C), BF),
        [SM, VM, VM, VM, VM],
        [
            pltpu.VMEM((2, 8 * CP, 3 * C), BF),
            pltpu.VMEM((2, F, 4 * CP, 2 * C), BF),
        ],
        flops=4 * 10**9,
    )(counts, part, prior, wide, upw)
    grad = call(
        kern(latent_grad_kernel), sd((F, BR, BW, C), F32), [SM, VM, VM, VM, VM, VM]
    )(counts, lat, gain, mine, from_above, from_below)
    return (decoded[:, None], grad[:, None])


def solution(mesh):
    blocks = P("section", "tile", None, None, None)
    return jax.shard_map(
        per_device,
        mesh=mesh,
        in_specs=(blocks, P(), P(), P(), P(), blocks),
        out_specs=(blocks, blocks),
        check_vma=False,
    )
```

```python
import functools

import jax
import jax.numpy as jnp
from jax import lax
from jax.experimental import pallas as pl
from jax.experimental.pallas import tpu as pltpu
from jax.sharding import PartitionSpec as P

GCOL = 4
EPS = 1e-06
F, BR, BW, C, CP = 4, 4, 24, 384, 32
BF, F32 = jnp.bfloat16, jnp.float32
NT = (((1,), (1,)), ((), ()))
VM = pl.BlockSpec(memory_space=pltpu.VMEM)
SM = pl.BlockSpec(memory_space=pltpu.SMEM)
ANY = pl.BlockSpec(memory_space=pl.ANY)


def place_of(axis_sizes):
    sections, tiles = axis_sizes
    at = lax.rem(lax.axis_index("tile") + GCOL + 1, tiles)
    row, col = lax.div(at, GCOL), lax.rem(at, GCOL)
    section = lax.axis_index("section")
    return dict(
        section=section,
        up=row > 0,
        down=row < tiles // GCOL - 1,
        first_below=lax.rem(row, 2) == 0,
        first_left=lax.rem(col, 2) == 0,
        left=col > 0,
        right=col < GCOL - 1,
        before=section > 0,
        after=section < sections - 1,
    )


def column_mask(where, width, valid):
    column = lax.broadcasted_iota(jnp.int32, (1, CP, C), 1)
    own = column < BW
    right = (column >= BW) & (column < BW + valid) & where["right"]
    left = (column >= CP - valid) & where["left"]
    return own | right | left


def activate(values, gain):
    scale = lax.rsqrt(jnp.mean(values * values, axis=-1, keepdims=True) + EPS)
    normed = values * scale * gain
    return normed * jax.nn.sigmoid(normed)


def shifted(x, by):
    return pltpu.roll(x, (-by) % CP, axis=x.ndim - 2)


def strips_kernel(sizes, lat, pg, one, two):
    even = place_of(sizes)["first_left"]
    for f in range(F):
        for source, base in ((lat, 0), (pg, BR * F)):
            rows = source.shape[1]
            first = source[f, :, 0:8].astype(F32)
            last = source[f, :, BW - 8 : BW].astype(F32)
            for k in range(2):
                a, b = first[:, k], last[:, 6 + k]
                to = slice(base + f * rows, base + (f + 1) * rows)
                one[k, to] = jnp.where(even, b, a).astype(BF)
                two[k, to] = jnp.where(even, a, b).astype(BF)


def side_columns(where, one, two, base, rows):
    even = where["first_left"]
    column = lax.broadcasted_iota(jnp.int32, (1, 8, C), 1)
    whole = jnp.zeros((rows, 8, C), F32)
    for k in range(2):
        a = one[k, base : base + rows].astype(F32)[:, None]
        b = two[k, base : base + rows].astype(F32)[:, None]
        whole = jnp.where(column == k, jnp.where(even, a, b), whole)
        whole = jnp.where(column == 6 + k, jnp.where(even, b, a), whole)
    return whole


def acts_kernel(sizes, lat, side_one, side_two, gain, out, one, two):
    where = place_of(sizes)
    mask = column_mask(where, C, 2)
    g = gain[...].reshape(1, 1, C)
    for f in range(F):
        side = side_columns(where, side_one, side_two, f * BR, BR)
        whole = jnp.concatenate([lat[f].astype(F32), side], axis=1)
        out[f] = jnp.where(mask, activate(whole, g), 0.0).astype(BF)
    start = jnp.where(where["first_below"], 2, 0)
    for f in range(F):
        one[f] = out[f, pl.ds(start, 2)]
        two[f] = out[f, pl.ds(2 - start, 2)]


def from_rows(where, one, two):
    below = where["first_below"]
    return jnp.where(below, two, one), jnp.where(below, one, two)


def up_taps(up, upw):
    rows = (((1, 2), (0,)), ((0, 1), (2,)))
    columns = ((1, 2), (0, 1), (0,), (2,))
    for k in range(2):
        for a in range(2):
            sums = [sum(up[dr, dc].astype(F32) for dr in rows[k][a]) for dc in range(3)]
            for b in range(4):
                total = sum(sums[dc] for dc in columns[b])
                upw[k, b * (C // 2) : (b + 1) * (C // 2), a * C : (a + 1) * C] = total.astype(BF)


def grad_hidden_kernel(sizes, counts, pg, rim_one, rim_two, up, own, out, upw, parts, acc):
    where = place_of(sizes)
    up_taps(up, upw)
    length = counts[where["section"]]
    mask = column_mask(where, C, 2)
    low = lax.broadcasted_iota(jnp.int32, (1, CP, C), 2) < C // 2
    for f in range(F):
        side = side_columns(where, rim_one, rim_two, BR * F + f * 2 * BR, 2 * BR)
        for r in range(0, 2 * BR, 2):
            whole = jnp.concatenate([pg[f, r : r + 2].astype(F32), side[r : r + 2]], axis=1)
            whole = jnp.where(mask & (f < length), whole, 0.0)
            mix = jnp.where(low, shifted(whole, 1), shifted(whole, -1))
            for k in range(2):
                rows = slice((r // 2) * CP, (r // 2 + 1) * CP)
                parts[k, f, rows, 0:C] = whole[k].astype(BF)
                parts[k, f, rows, C : 2 * C] = mix[k].astype(BF)
    even = parts[0].reshape(F * BR * CP, 2 * C)
    odd = parts[1].reshape(F * BR * CP, 2 * C)

    def term(x, k, a):
        taps = upw[k, :, a * C : (a + 1) * C]
        return jnp.dot(x, taps, preferred_element_type=F32).reshape(F, BR * CP, C)

    acc[:, CP : 5 * CP] = term(even, 0, 0) + term(odd, 1, 0)
    acc[:, 0:CP] = jnp.zeros((F, CP, C), F32)
    acc[:, 5 * CP : 6 * CP] = jnp.zeros((F, CP, C), F32)
    acc[:, 0 : 4 * CP] += term(even, 0, 1)
    acc[:, 2 * CP : 6 * CP] += term(odd, 1, 1)
    inner = column_mask(where, C, 1)
    for f in range(F):
        value = acc[f].reshape(6, CP, C)
        row = lax.broadcasted_iota(jnp.int32, (6, CP, C), 0)
        keep = inner & ((row > 0) | where["up"]) & ((row < 5) | where["down"])
        out[f] = jnp.where(keep, value, 0.0).astype(BF)


def back_kernel(gh, weight, acc_out, early_out, cells, acc):
    for f in range(F):
        value = gh[f].astype(F32)
        for dc in range(3):
            moved = value if dc == 1 else shifted(value, 1 - dc)
            cells[f, :, dc * C : (dc + 1) * C] = moved[:, 0:BW].reshape(6 * BW, C).astype(BF)
    acc[...] = jnp.zeros(acc.shape, F32)
    left = cells[...].reshape(F * 6 * BW, 3 * C)
    for dt in (2, 1, 0):
        taps = jnp.concatenate(
            [
                jnp.concatenate([weight[dt, dr, dc] for dc in range(3)], axis=1)
                for dr in range(3)
            ],
            axis=0,
        )
        product = lax.dot_general(left, taps, NT, preferred_element_type=F32)
        for dr in range(3):
            for f in range(F):
                acc[f + dt, dr * BW : (dr + 6) * BW] += product[
                    f * 6 * BW : (f + 1) * 6 * BW, dr * C : (dr + 1) * C
                ]
    early_out[...] = acc[0:2].astype(BF)
    acc_out[...] = acc[2:6]


def edge_frames_kernel(sizes, counts, own, one, two, early, out):
    where = place_of(sizes)
    length = counts[where["section"]]
    for k in range(2):
        f = length - 2 + k
        above, below = from_rows(where, one[f], two[f])
        out[k, 0:2] = jnp.where(where["up"], above, jnp.zeros((2, CP, C), BF))
        out[k, 2:6] = own[f]
        out[k, 6:8] = jnp.where(where["down"], below, jnp.zeros((2, CP, C), BF))


def side_by_side(x, rows, cells, f):
    for dc in range(3):
        moved = x if dc == 1 else shifted(x, dc - 1)
        count = x.shape[0] * CP
        cells[f, rows * CP : rows * CP + count, dc * C : (dc + 1) * C] = moved.reshape(
            count, C
        ).astype(BF)


def forward_own_kernel(own, weight, edge, acc, cells):
    for f in range(F):
        side_by_side(own[f].astype(F32), 0, cells, f)
    acc[...] = jnp.zeros(acc.shape, F32)
    for dt in (2, 1, 0):
        count = F - (2 - dt)
        taps = jnp.concatenate([weight[dt, dr] for dr in range(3)], axis=1)
        left = cells[0:count].reshape(count * BR * CP, 3 * C)
        product = jnp.dot(left, taps, preferred_element_type=F32)
        for dr in range(3):
            for f in range(count):
                acc[f + 2 - dt, (2 - dr) * CP : (6 - dr) * CP] += product[
                    f * BR * CP : (f + 1) * BR * CP, dr * C : (dr + 1) * C
                ]


def forward_rim_kernel(sizes, one, two, part, weight, mine, acc, cells):
    where = place_of(sizes)
    for f in range(F):
        above, below = from_rows(where, one[f].astype(F32), two[f].astype(F32))
        side_by_side(jnp.where(where["up"], above, 0.0), 0, cells, f)
        side_by_side(jnp.where(where["down"], below, 0.0), 2, cells, f)
    acc[...] = part[...]
    for dt in (2, 1, 0):
        count = F - (2 - dt)
        terms = []
        for dr in range(3):
            left = cells[0:count, dr * CP : (dr + 2) * CP].reshape(count * 2 * CP, 3 * C)
            term = jnp.dot(left, weight[dt, dr], preferred_element_type=F32)
            terms.append(term.reshape(count, 2 * CP, C))
        acc[2 - dt : F, 0 : 2 * CP] += terms[0]
        acc[2 - dt : F, 0:CP] += terms[1][:, 0:CP]
        acc[2 - dt : F, 5 * CP : 6 * CP] += terms[1][:, CP : 2 * CP]
        acc[2 - dt : F, 4 * CP : 6 * CP] += terms[2]


def decode_kernel(sizes, counts, part, prior, weight, upw, out, mark, cells, pairs):
    where = place_of(sizes)
    length = counts[where["section"]]
    for k in range(2):
        side_by_side(jnp.where(where["before"], prior[k].astype(F32), 0.0), 0, cells, k)

    def term(first, count, dt):
        total = None
        for dr in range(3):
            left = cells[first : first + count, dr * CP : (dr + 6) * CP].reshape(count * 6 * CP, 3 * C)
            value = jnp.dot(left, weight[dt, dr], preferred_element_type=F32)
            total = value if total is None else total + value
        return total.reshape(count, 6 * CP, C)

    early = part[0:2] + term(0, 2, 0)
    late = term(1, 1, 1)
    inner = column_mask(where, C, 1)
    row = lax.broadcasted_iota(jnp.int32, (6, CP, C), 0)
    keep = inner & ((row > 0) | where["up"]) & ((row < 5) | where["down"])
    for f in range(F):
        value = part[f] if f >= 2 else early[f]
        if f == 0:
            value = value + late[0]
        hidden = jnp.where(keep, value.reshape(6, CP, C), 0.0).reshape(6 * CP, C).astype(BF)
        pairs[0, f, :, 0:C] = hidden[CP : 5 * CP]
        pairs[0, f, :, C : 2 * C] = hidden[0 : 4 * CP]
        pairs[1, f, :, 0:C] = hidden[CP : 5 * CP]
        pairs[1, f, :, C : 2 * C] = hidden[2 * CP : 6 * CP]
    low = lax.broadcasted_iota(jnp.int32, (1, CP, C), 2) < C // 2
    for k in range(2):
        rows = lax.dot_general(
            pairs[k].reshape(F * 4 * CP, 2 * C), upw[k], NT, preferred_element_type=F32
        )
        for f in range(F):
            whole = rows[f * 4 * CP : (f + 1) * 4 * CP].reshape(4, CP, 2 * C)
            side = whole[:, :, C : 2 * C]
            mix = jnp.where(low, shifted(side, -1), shifted(side, 1))
            value = jnp.where(f < length, whole[:, :, 0:C] + mix, 0.0)[:, 0:BW].astype(BF)
            for r in range(BR):
                out[f, 2 * r + k] = value[r]
    mark[...] = jnp.zeros(mark.shape, F32)


def later_group_kernel(sizes, counts, acc, later, one, two, own, total):
    where = place_of(sizes)
    length = counts[where["section"]]
    total[...] = acc[...]
    for k in range(2):
        f = length - 2 + k
        total[f] += jnp.where(where["after"], later[k].astype(F32), 0.0)
    top, bottom = total[:, 0 : 2 * BW], total[:, 6 * BW : 8 * BW]
    below = where["first_below"]
    one[...] = jnp.where(below, bottom, top).astype(BF)
    two[...] = jnp.where(below, top, bottom).astype(BF)
    own[...] = total[:, 2 * BW : 6 * BW]


def latent_grad_kernel(sizes, counts, lat, gain, own, one, two, mark, out):
    where = place_of(sizes)
    length = counts[where["section"]]
    g = gain[...].reshape(1, 1, C)
    for f in range(F):
        x = lat[f].astype(F32)
        above, below = from_rows(where, one[f].astype(F32), two[f].astype(F32))
        upper = own[f, 0 : 2 * BW] + jnp.where(where["up"], above, 0.0)
        lower = own[f, 2 * BW : 4 * BW] + jnp.where(where["down"], below, 0.0)
        grad = jnp.concatenate([upper, lower], 0).reshape(BR, BW, C)
        scale = lax.rsqrt(jnp.mean(x * x, axis=-1, keepdims=True) + EPS)
        unit = x * scale
        v = unit * g
        s = jax.nn.sigmoid(v)
        t = grad * (s + v * s * (1.0 - s)) * g
        slope = jnp.mean(t * unit, axis=-1, keepdims=True)
        out[f] = jnp.where(f < length, scale * (t - unit * slope), 0.0)


def call(kernel, outs, ins, scratch=(), flops=0, limit=40, outs_at=None, aliases=None):
    return pl.pallas_call(
        kernel,
        out_shape=outs,
        in_specs=ins,
        out_specs=outs_at or jax.tree.map(lambda _: VM, outs),
        scratch_shapes=list(scratch),
        input_output_aliases=aliases or {},
        compiler_params=pltpu.CompilerParams(vmem_limit_bytes=limit * 2**20),
        cost_estimate=pl.CostEstimate(flops=flops, bytes_accessed=1000000, transcendentals=0),
    )


def ring(value, axis, steps):
    count = lax.axis_size(axis)
    return lax.ppermute(value, axis, [(i, (i + steps) % count) for i in range(count)])


def swap(value, tiles, unit, second):
    shift = GCOL + 1 + second * unit
    return lax.ppermute(
        value, "tile", [(at, (((at + shift) ^ unit) - shift) % tiles) for at in range(tiles)]
    )


def per_device(latents, counts, norm_gain, conv_weight, up_weight, pixel_grad):
    sizes = (lax.axis_size("section"), lax.axis_size("tile"))
    lat, pg = latents[:, 0], pixel_grad[:, 0]
    gain = norm_gain.reshape(1, C)
    sd = jax.ShapeDtypeStruct
    kern = lambda k: functools.partial(k, sizes)
    wide = conv_weight.reshape(3, 3, 3 * C, C)

    tiles = sizes[1]
    side = sd((2, 3 * BR * F, C), BF)
    side_one, side_two = call(kern(strips_kernel), (side, side), [VM, VM], flops=4 * 10**9)(lat, pg)
    side_one, side_two = swap(side_one, tiles, 1, 0), swap(side_two, tiles, 1, 1)
    rim = sd((F, 2, CP, C), BF)
    own, one, two = call(
        kern(acts_kernel), (sd((F, BR, CP, C), BF), rim, rim), [VM, VM, VM, VM], flops=4 * 10**9
    )(lat, side_one, side_two, gain)
    one, two = swap(one, tiles, GCOL, 0), swap(two, tiles, GCOL, 1)
    gh, upw = call(
        kern(grad_hidden_kernel),
        (sd((F, 6, CP, C), BF), sd((2, 2 * C, 2 * C), BF)),
        [SM, VM, VM, VM, VM, ANY],
        [pltpu.VMEM((2, F, BR * CP, 2 * C), BF), pltpu.VMEM((F, 6 * CP, C), F32)],
        flops=3 * 10**9,
    )(counts, pg, side_one, side_two, jnp.transpose(up_weight, (0, 1, 3, 2)), own)
    acc, early = call(
        back_kernel,
        (sd((F, 8 * BW, C), F32), sd((2, 8 * BW, C), BF)),
        [VM, VM],
        [
            pltpu.VMEM((F, 6 * BW, 3 * C), BF),
            pltpu.VMEM((F + 2, 8 * BW, C), F32),
        ],
        flops=6 * 10**9,
    )(gh, conv_weight)
    edge = call(
        kern(edge_frames_kernel), sd((2, 8, CP, C), BF), [SM, VM, VM, VM, ANY]
    )(counts, own, one, two, early)
    prior = ring(edge, "section", 1)
    later = ring(early, "section", -1)
    partial = sd((F, 6 * CP, C), F32)
    part = call(
        forward_own_kernel,
        partial,
        [VM, VM, ANY],
        [pltpu.VMEM((F, BR * CP, 3 * C), BF)],
        flops=4 * 10**9,
    )(own, wide, edge)
    rims = one, two
    one, two, mine = call(
        kern(later_group_kernel),
        (sd((F, 2 * BW, C), BF), sd((F, 2 * BW, C), BF), sd((F, 4 * BW, C), F32)),
        [SM, VM, VM],
        [pltpu.VMEM((F, 8 * BW, C), F32)],
    )(counts, acc, later)
    one, two = swap(one, tiles, GCOL, 0), swap(two, tiles, GCOL, 1)
    part = call(
        kern(forward_rim_kernel),
        partial,
        [VM, VM, VM, VM, ANY],
        [pltpu.VMEM((F, BR * CP, 3 * C), BF)],
        flops=3 * 10**9,
    )(*rims, part, wide, mine)
    decoded, mark = call(
        kern(decode_kernel),
        (sd((F, 2 * BR, BW, C), BF), sd((8, 128), F32)),
        [SM, VM, VM, VM, VM],
        [
            pltpu.VMEM((2, 8 * CP, 3 * C), BF),
            pltpu.VMEM((2, F, 4 * CP, 2 * C), BF),
        ],
        flops=4 * 10**9,
    )(counts, part, prior, wide, upw)
    grad = call(
        kern(latent_grad_kernel), sd((F, BR, BW, C), F32), [SM, VM, VM, VM, VM, VM, ANY]
    )(counts, lat, gain, mine, one, two, mark)
    return (decoded[:, None], grad[:, None])


def solution(mesh):
    blocks = P("section", "tile", None, None, None)
    return jax.shard_map(
        per_device,
        mesh=mesh,
        in_specs=(blocks, P(), P(), P(), P(), blocks),
        out_specs=(blocks, blocks),
        check_vma=False,
    )
```

```python
import functools

import jax
import jax.numpy as jnp
from jax import lax
from jax.experimental import pallas as pl
from jax.experimental.pallas import tpu as pltpu
from jax.sharding import PartitionSpec as P

GCOL = 4
EPS = 1e-06
F, BR, BW, C, CP = 4, 4, 24, 384, 32
BF, F32 = jnp.bfloat16, jnp.float32
NT = (((1,), (1,)), ((), ()))
VM = pl.BlockSpec(memory_space=pltpu.VMEM)
SM = pl.BlockSpec(memory_space=pltpu.SMEM)
ANY = pl.BlockSpec(memory_space=pl.ANY)


def place_of(axis_sizes):
    sections, tiles = axis_sizes
    at = lax.rem(lax.axis_index("tile") + GCOL + 1, tiles)
    row, col = lax.div(at, GCOL), lax.rem(at, GCOL)
    section = lax.axis_index("section")
    return dict(
        section=section,
        up=row > 0,
        down=row < tiles // GCOL - 1,
        first_below=lax.rem(row, 2) == 0,
        first_left=lax.rem(col, 2) == 0,
        left=col > 0,
        right=col < GCOL - 1,
        before=section > 0,
        after=section < sections - 1,
    )


def column_mask(where, width, valid):
    column = lax.broadcasted_iota(jnp.int32, (1, CP, C), 1)
    own = column < BW
    right = (column >= BW) & (column < BW + valid) & where["right"]
    left = (column >= CP - valid) & where["left"]
    return own | right | left


def activate(values, gain):
    scale = lax.rsqrt(jnp.mean(values * values, axis=-1, keepdims=True) + EPS)
    normed = values * scale * gain
    return normed * jax.nn.sigmoid(normed)


def shifted(x, by):
    return pltpu.roll(x, (-by) % CP, axis=x.ndim - 2)


def strips_kernel(sizes, lat, pg, one, two):
    even = place_of(sizes)["first_left"]
    for f in range(F):
        for source, base in ((lat, 0), (pg, BR * F)):
            rows = source.shape[1]
            first = source[f, :, 0:8].astype(F32)
            last = source[f, :, BW - 8 : BW].astype(F32)
            for k in range(2):
                a, b = first[:, k], last[:, 6 + k]
                to = slice(base + f * rows, base + (f + 1) * rows)
                one[k, to] = jnp.where(even, b, a).astype(BF)
                two[k, to] = jnp.where(even, a, b).astype(BF)


def side_columns(where, one, two, base, rows):
    even = where["first_left"]
    column = lax.broadcasted_iota(jnp.int32, (1, 8, C), 1)
    whole = jnp.zeros((rows, 8, C), F32)
    for k in range(2):
        a = one[k, base : base + rows].astype(F32)[:, None]
        b = two[k, base : base + rows].astype(F32)[:, None]
        whole = jnp.where(column == k, jnp.where(even, a, b), whole)
        whole = jnp.where(column == 6 + k, jnp.where(even, b, a), whole)
    return whole


def acts_kernel(sizes, lat, side_one, side_two, gain, out, one, two):
    where = place_of(sizes)
    mask = column_mask(where, C, 2)
    g = gain[...].reshape(1, 1, C)
    for f in range(F):
        side = side_columns(where, side_one, side_two, f * BR, BR)
        whole = jnp.concatenate([lat[f].astype(F32), side], axis=1)
        out[f] = jnp.where(mask, activate(whole, g), 0.0).astype(BF)
    start = jnp.where(where["first_below"], 2, 0)
    for f in range(F):
        one[f] = packed(out[f, pl.ds(start, 2)].astype(F32)).astype(BF)
        two[f] = packed(out[f, pl.ds(2 - start, 2)].astype(F32)).astype(BF)


def side_places():
    place = lax.broadcasted_iota(jnp.int32, (8, C), 0)
    return (place < 2) | (place >= 6)


def packed(rows):
    own = rows[:, 0:BW].reshape(2 * BW, C)
    side = jnp.where(side_places(), rows[0, BW:CP], pltpu.roll(rows[1, BW:CP], 4, axis=0))
    return jnp.concatenate([own, side], axis=0)


def unpacked(block):
    own, side = block[0 : 2 * BW].reshape(2, BW, C), block[2 * BW :]
    sides = [jnp.where(side_places(), x, 0.0) for x in (side, pltpu.roll(side, 4, axis=0))]
    return jnp.concatenate([own, jnp.stack(sides, 0)], axis=1)


def from_rows(where, one, two):
    below = where["first_below"]
    return jnp.where(below, two, one), jnp.where(below, one, two)


def up_taps(up, upw):
    rows = (((1, 2), (0,)), ((0, 1), (2,)))
    columns = ((1, 2), (0, 1), (0,), (2,))
    for k in range(2):
        for a in range(2):
            sums = [sum(up[dr, dc].astype(F32) for dr in rows[k][a]) for dc in range(3)]
            for b in range(4):
                total = sum(sums[dc] for dc in columns[b])
                upw[k, b * (C // 2) : (b + 1) * (C // 2), a * C : (a + 1) * C] = total.astype(BF)


def grad_hidden_kernel(sizes, counts, pg, rim_one, rim_two, up, own, out, upw, parts, acc):
    where = place_of(sizes)
    up_taps(up, upw)
    length = counts[where["section"]]
    mask = column_mask(where, C, 2)
    low = lax.broadcasted_iota(jnp.int32, (1, CP, C), 2) < C // 2
    for f in range(F):
        side = side_columns(where, rim_one, rim_two, BR * F + f * 2 * BR, 2 * BR)
        for r in range(0, 2 * BR, 2):
            whole = jnp.concatenate([pg[f, r : r + 2].astype(F32), side[r : r + 2]], axis=1)
            whole = jnp.where(mask & (f < length), whole, 0.0)
            mix = jnp.where(low, shifted(whole, 1), shifted(whole, -1))
            for k in range(2):
                rows = slice((r // 2) * CP, (r // 2 + 1) * CP)
                parts[k, f, rows, 0:C] = whole[k].astype(BF)
                parts[k, f, rows, C : 2 * C] = mix[k].astype(BF)
    even = parts[0].reshape(F * BR * CP, 2 * C)
    odd = parts[1].reshape(F * BR * CP, 2 * C)

    def term(x, k, a):
        taps = upw[k, :, a * C : (a + 1) * C]
        return jnp.dot(x, taps, preferred_element_type=F32).reshape(F, BR * CP, C)

    acc[:, CP : 5 * CP] = term(even, 0, 0) + term(odd, 1, 0)
    acc[:, 0:CP] = jnp.zeros((F, CP, C), F32)
    acc[:, 5 * CP : 6 * CP] = jnp.zeros((F, CP, C), F32)
    acc[:, 0 : 4 * CP] += term(even, 0, 1)
    acc[:, 2 * CP : 6 * CP] += term(odd, 1, 1)
    inner = column_mask(where, C, 1)
    for f in range(F):
        value = acc[f].reshape(6, CP, C)
        row = lax.broadcasted_iota(jnp.int32, (6, CP, C), 0)
        keep = inner & ((row > 0) | where["up"]) & ((row < 5) | where["down"])
        out[f] = jnp.where(keep, value, 0.0).astype(BF)


def back_kernel(gh, weight, acc_out, early_out, cells, acc):
    for f in range(F):
        value = gh[f].astype(F32)
        for dc in range(3):
            moved = value if dc == 1 else shifted(value, 1 - dc)
            cells[f, :, dc * C : (dc + 1) * C] = moved[:, 0:BW].reshape(6 * BW, C).astype(BF)
    acc[...] = jnp.zeros(acc.shape, F32)
    left = cells[...].reshape(F * 6 * BW, 3 * C)
    for dt in (2, 1, 0):
        taps = jnp.concatenate(
            [
                jnp.concatenate([weight[dt, dr, dc] for dc in range(3)], axis=1)
                for dr in range(3)
            ],
            axis=0,
        )
        product = lax.dot_general(left, taps, NT, preferred_element_type=F32)
        for dr in range(3):
            for f in range(F):
                acc[f + dt, dr * BW : (dr + 6) * BW] += product[
                    f * 6 * BW : (f + 1) * 6 * BW, dr * C : (dr + 1) * C
                ]
    early_out[...] = acc[0:2].astype(BF)
    acc_out[...] = acc[2:6]


def edge_frames_kernel(sizes, counts, own, one, two, early, out):
    where = place_of(sizes)
    length = counts[where["section"]]
    for k in range(2):
        f = length - 2 + k
        above, below = from_rows(where, one[f].astype(F32), two[f].astype(F32))
        out[k, 0] = jnp.where(where["up"], above, 0.0).astype(BF)
        for r in range(2):
            out[k, 1 + r] = packed(own[f, 2 * r : 2 * r + 2].astype(F32)).astype(BF)
        out[k, 3] = jnp.where(where["down"], below, 0.0).astype(BF)


def side_by_side(x, rows, cells, f):
    for dc in range(3):
        moved = x if dc == 1 else shifted(x, dc - 1)
        count = x.shape[0] * CP
        cells[f, rows * CP : rows * CP + count, dc * C : (dc + 1) * C] = moved.reshape(
            count, C
        ).astype(BF)


def forward_own_kernel(own, weight, edge, acc, cells):
    for f in range(F):
        side_by_side(own[f].astype(F32), 0, cells, f)
    acc[...] = jnp.zeros(acc.shape, F32)
    for dt in (2, 1, 0):
        count = F - (2 - dt)
        taps = jnp.concatenate([weight[dt, dr] for dr in range(3)], axis=1)
        left = cells[0:count].reshape(count * BR * CP, 3 * C)
        product = jnp.dot(left, taps, preferred_element_type=F32)
        for dr in range(3):
            for f in range(count):
                acc[f + 2 - dt, (2 - dr) * CP : (6 - dr) * CP] += product[
                    f * BR * CP : (f + 1) * BR * CP, dr * C : (dr + 1) * C
                ]


def forward_rim_kernel(sizes, one, two, part, weight, mine, acc, cells):
    where = place_of(sizes)
    for f in range(F):
        above, below = from_rows(where, one[f].astype(F32), two[f].astype(F32))
        side_by_side(jnp.where(where["up"], unpacked(above), 0.0), 0, cells, f)
        side_by_side(jnp.where(where["down"], unpacked(below), 0.0), 2, cells, f)
    acc[...] = part[...]
    for dt in (2, 1, 0):
        count = F - (2 - dt)
        terms = []
        for dr in range(3):
            left = cells[0:count, dr * CP : (dr + 2) * CP].reshape(count * 2 * CP, 3 * C)
            term = jnp.dot(left, weight[dt, dr], preferred_element_type=F32)
            terms.append(term.reshape(count, 2 * CP, C))
        acc[2 - dt : F, 0 : 2 * CP] += terms[0]
        acc[2 - dt : F, 0:CP] += terms[1][:, 0:CP]
        acc[2 - dt : F, 5 * CP : 6 * CP] += terms[1][:, CP : 2 * CP]
        acc[2 - dt : F, 4 * CP : 6 * CP] += terms[2]


def decode_kernel(sizes, counts, part, prior, weight, upw, out_hbm, mark, cells, pairs, out, sems):
    where = place_of(sizes)
    length = counts[where["section"]]
    for k in range(2):
        for r in range(4):
            rows = jnp.where(where["before"], unpacked(prior[k, r].astype(F32)), 0.0)
            side_by_side(rows, 2 * r, cells, k)

    def term(first, count, dt):
        total = None
        for dr in range(3):
            left = cells[first : first + count, dr * CP : (dr + 6) * CP].reshape(count * 6 * CP, 3 * C)
            value = jnp.dot(left, weight[dt, dr], preferred_element_type=F32)
            total = value if total is None else total + value
        return total.reshape(count, 6 * CP, C)

    early = part[0:2] + term(0, 2, 0)
    late = term(1, 1, 1)
    inner = column_mask(where, C, 1)
    row = lax.broadcasted_iota(jnp.int32, (6, CP, C), 0)
    keep = inner & ((row > 0) | where["up"]) & ((row < 5) | where["down"])
    for f in range(F):
        value = part[f] if f >= 2 else early[f]
        if f == 0:
            value = value + late[0]
        hidden = jnp.where(keep, value.reshape(6, CP, C), 0.0).reshape(6 * CP, C).astype(BF)
        pairs[0, f, :, 0:C] = hidden[CP : 5 * CP]
        pairs[0, f, :, C : 2 * C] = hidden[0 : 4 * CP]
        pairs[1, f, :, 0:C] = hidden[CP : 5 * CP]
        pairs[1, f, :, C : 2 * C] = hidden[2 * CP : 6 * CP]
    low = lax.broadcasted_iota(jnp.int32, (1, CP, C), 2) < C // 2
    products = [
        lax.dot_general(
            pairs[k].reshape(F * 4 * CP, 2 * C), upw[k], NT, preferred_element_type=F32
        )
        for k in range(2)
    ]
    copies = []
    for f in range(F):
        for k in range(2):
            whole = products[k][f * 4 * CP : (f + 1) * 4 * CP].reshape(4, CP, 2 * C)
            side = whole[:, :, C : 2 * C]
            mix = jnp.where(low, shifted(side, -1), shifted(side, 1))
            value = jnp.where(f < length, whole[:, :, 0:C] + mix, 0.0)[:, 0:BW].astype(BF)
            for r in range(BR):
                out[f, 2 * r + k] = value[r]
        copies.append(pltpu.make_async_copy(out.at[f], out_hbm.at[f], sems.at[f]))
        copies[f].start()
    mark[...] = jnp.zeros(mark.shape, F32)
    for copy in copies:
        copy.wait()


def later_group_kernel(sizes, counts, acc, later, one, two, own, total):
    where = place_of(sizes)
    length = counts[where["section"]]
    total[...] = acc[...]
    for k in range(2):
        f = length - 2 + k
        total[f] += jnp.where(where["after"], later[k].astype(F32), 0.0)
    top, bottom = total[:, 0 : 2 * BW], total[:, 6 * BW : 8 * BW]
    below = where["first_below"]
    one[...] = jnp.where(below, bottom, top).astype(BF)
    two[...] = jnp.where(below, top, bottom).astype(BF)
    own[...] = total[:, 2 * BW : 6 * BW]


def latent_grad_kernel(sizes, counts, lat, gain, own, one, two, mark, out_hbm, out, sems):
    where = place_of(sizes)
    length = counts[where["section"]]
    g = gain[...].reshape(1, 1, C)
    copies = []
    for f in range(F):
        x = lat[f].astype(F32)
        above, below = from_rows(where, one[f].astype(F32), two[f].astype(F32))
        upper = own[f, 0 : 2 * BW] + jnp.where(where["up"], above, 0.0)
        lower = own[f, 2 * BW : 4 * BW] + jnp.where(where["down"], below, 0.0)
        grad = jnp.concatenate([upper, lower], 0).reshape(BR, BW, C)
        scale = lax.rsqrt(jnp.mean(x * x, axis=-1, keepdims=True) + EPS)
        unit = x * scale
        v = unit * g
        s = jax.nn.sigmoid(v)
        t = grad * (s + v * s * (1.0 - s)) * g
        slope = jnp.mean(t * unit, axis=-1, keepdims=True)
        out[f] = jnp.where(f < length, scale * (t - unit * slope), 0.0)
        copies.append(pltpu.make_async_copy(out.at[f], out_hbm.at[f], sems.at[f]))
        copies[f].start()
    for copy in copies:
        copy.wait()


def call(kernel, outs, ins, scratch=(), flops=0, limit=40, outs_at=None, aliases=None):
    return pl.pallas_call(
        kernel,
        out_shape=outs,
        in_specs=ins,
        out_specs=outs_at or jax.tree.map(lambda _: VM, outs),
        scratch_shapes=list(scratch),
        input_output_aliases=aliases or {},
        compiler_params=pltpu.CompilerParams(vmem_limit_bytes=limit * 2**20),
        cost_estimate=pl.CostEstimate(flops=flops, bytes_accessed=1000000, transcendentals=0),
    )


def ring(value, axis, steps):
    count = lax.axis_size(axis)
    return lax.ppermute(value, axis, [(i, (i + steps) % count) for i in range(count)])


def swap(value, tiles, unit, second):
    shift = GCOL + 1 + second * unit
    return lax.ppermute(
        value, "tile", [(at, (((at + shift) ^ unit) - shift) % tiles) for at in range(tiles)]
    )


def per_device(latents, counts, norm_gain, conv_weight, up_weight, pixel_grad):
    sizes = (lax.axis_size("section"), lax.axis_size("tile"))
    lat, pg = latents[:, 0], pixel_grad[:, 0]
    gain = norm_gain.reshape(1, C)
    sd = jax.ShapeDtypeStruct
    kern = lambda k: functools.partial(k, sizes)
    wide = conv_weight.reshape(3, 3, 3 * C, C)

    tiles = sizes[1]
    side = sd((2, 3 * BR * F, C), BF)
    side_one, side_two = call(kern(strips_kernel), (side, side), [VM, VM], flops=4 * 10**9)(lat, pg)
    side_one, side_two = swap(side_one, tiles, 1, 0), swap(side_two, tiles, 1, 1)
    rim = sd((F, 2 * BW + 8, C), BF)
    own, one, two = call(
        kern(acts_kernel), (sd((F, BR, CP, C), BF), rim, rim), [VM, VM, VM, VM], flops=4 * 10**9
    )(lat, side_one, side_two, gain)
    one, two = swap(one, tiles, GCOL, 0), swap(two, tiles, GCOL, 1)
    gh, upw = call(
        kern(grad_hidden_kernel),
        (sd((F, 6, CP, C), BF), sd((2, 2 * C, 2 * C), BF)),
        [SM, VM, VM, VM, VM, ANY],
        [pltpu.VMEM((2, F, BR * CP, 2 * C), BF), pltpu.VMEM((F, 6 * CP, C), F32)],
        flops=3 * 10**9,
    )(counts, pg, side_one, side_two, jnp.transpose(up_weight, (0, 1, 3, 2)), own)
    acc, early = call(
        back_kernel,
        (sd((F, 8 * BW, C), F32), sd((2, 8 * BW, C), BF)),
        [VM, VM],
        [
            pltpu.VMEM((F, 6 * BW, 3 * C), BF),
            pltpu.VMEM((F + 2, 8 * BW, C), F32),
        ],
        flops=6 * 10**9,
    )(gh, conv_weight)
    edge = call(
        kern(edge_frames_kernel), sd((2, 4, 2 * BW + 8, C), BF), [SM, VM, VM, VM, ANY]
    )(counts, own, one, two, early)
    prior = ring(edge, "section", 1)
    later = ring(early, "section", -1)
    partial = sd((F, 6 * CP, C), F32)
    part = call(
        forward_own_kernel,
        partial,
        [VM, VM, ANY],
        [pltpu.VMEM((F, BR * CP, 3 * C), BF)],
        flops=4 * 10**9,
    )(own, wide, edge)
    rims = one, two
    one, two, mine = call(
        kern(later_group_kernel),
        (sd((F, 2 * BW, C), BF), sd((F, 2 * BW, C), BF), sd((F, 4 * BW, C), F32)),
        [SM, VM, VM],
        [pltpu.VMEM((F, 8 * BW, C), F32)],
    )(counts, acc, later)
    one, two = swap(one, tiles, GCOL, 0), swap(two, tiles, GCOL, 1)
    part = call(
        kern(forward_rim_kernel),
        partial,
        [VM, VM, VM, VM, ANY],
        [pltpu.VMEM((F, BR * CP, 3 * C), BF)],
        flops=3 * 10**9,
    )(*rims, part, wide, mine)
    decoded, mark = call(
        kern(decode_kernel),
        (sd((F, 2 * BR, BW, C), BF), sd((8, 128), F32)),
        [SM, VM, VM, VM, VM],
        [
            pltpu.VMEM((2, 8 * CP, 3 * C), BF),
            pltpu.VMEM((2, F, 4 * CP, 2 * C), BF),
            pltpu.VMEM((F, 2 * BR, BW, C), BF),
            pltpu.SemaphoreType.DMA((F,)),
        ],
        outs_at=(ANY, VM),
        flops=4 * 10**9,
    )(counts, part, prior, wide, upw)
    grad = call(
        kern(latent_grad_kernel), sd((F, BR, BW, C), F32), [SM, VM, VM, VM, VM, VM, ANY],
        [pltpu.VMEM((F, BR, BW, C), F32), pltpu.SemaphoreType.DMA((F,))],
        outs_at=ANY,
    )(counts, lat, gain, mine, one, two, mark)
    return (decoded[:, None], grad[:, None])


def solution(mesh):
    blocks = P("section", "tile", None, None, None)
    return jax.shard_map(
        per_device,
        mesh=mesh,
        in_specs=(blocks, P(), P(), P(), P(), blocks),
        out_specs=(blocks, blocks),
        check_vma=False,
    )
```

```python
import functools

import jax
import jax.numpy as jnp
from jax import lax
from jax.experimental import pallas as pl
from jax.experimental.pallas import tpu as pltpu
from jax.sharding import PartitionSpec as P

GCOL = 4
EPS = 1e-06
F, BR, BW, C, CP = 4, 4, 24, 384, 32
BF, F32 = jnp.bfloat16, jnp.float32
NT = (((1,), (1,)), ((), ()))
VM = pl.BlockSpec(memory_space=pltpu.VMEM)
SM = pl.BlockSpec(memory_space=pltpu.SMEM)
ANY = pl.BlockSpec(memory_space=pl.ANY)


def place_of(axis_sizes):
    sections, tiles = axis_sizes
    at = lax.rem(lax.axis_index("tile") + GCOL + 1, tiles)
    row, col = lax.div(at, GCOL), lax.rem(at, GCOL)
    section = lax.axis_index("section")
    return dict(
        section=section,
        up=row > 0,
        down=row < tiles // GCOL - 1,
        first_below=lax.rem(row, 2) == 0,
        first_left=lax.rem(col, 2) == 0,
        left=col > 0,
        right=col < GCOL - 1,
        before=section > 0,
        after=section < sections - 1,
    )


def column_mask(where, width, valid):
    column = lax.broadcasted_iota(jnp.int32, (1, CP, C), 1)
    own = column < BW
    right = (column >= BW) & (column < BW + valid) & where["right"]
    left = (column >= CP - valid) & where["left"]
    return own | right | left


def activate(values, gain):
    scale = lax.rsqrt(jnp.mean(values * values, axis=-1, keepdims=True) + EPS)
    normed = values * scale * gain
    return normed * jax.nn.sigmoid(normed)


def shifted(x, by):
    return pltpu.roll(x, (-by) % CP, axis=x.ndim - 2)


def strips_kernel(sizes, lat, pg, one, two):
    even = place_of(sizes)["first_left"]
    for f in range(F):
        for source, base in ((lat, 0), (pg, BR * F)):
            rows = source.shape[1]
            first = source[f, :, 0:8].astype(F32)
            last = source[f, :, BW - 8 : BW].astype(F32)
            for k in range(2):
                a, b = first[:, k], last[:, 6 + k]
                to = slice(base + f * rows, base + (f + 1) * rows)
                one[k, to] = jnp.where(even, b, a).astype(BF)
                two[k, to] = jnp.where(even, a, b).astype(BF)


def side_columns(where, one, two, base, rows):
    even = where["first_left"]
    column = lax.broadcasted_iota(jnp.int32, (1, 8, C), 1)
    whole = jnp.zeros((rows, 8, C), F32)
    for k in range(2):
        a = one[k, base : base + rows].astype(F32)[:, None]
        b = two[k, base : base + rows].astype(F32)[:, None]
        whole = jnp.where(column == k, jnp.where(even, a, b), whole)
        whole = jnp.where(column == 6 + k, jnp.where(even, b, a), whole)
    return whole


def acts_kernel(sizes, lat, side_one, side_two, gain, out, one, two):
    where = place_of(sizes)
    mask = column_mask(where, C, 2)
    g = gain[...].reshape(1, 1, C)
    for f in range(F):
        side = side_columns(where, side_one, side_two, f * BR, BR)
        whole = jnp.concatenate([lat[f].astype(F32), side], axis=1)
        out[f] = jnp.where(mask, activate(whole, g), 0.0).astype(BF)
    start = jnp.where(where["first_below"], 2, 0)
    for f in range(F):
        one[f] = packed(out[f, pl.ds(start, 2)].astype(F32)).astype(BF)
        two[f] = packed(out[f, pl.ds(2 - start, 2)].astype(F32)).astype(BF)


def side_places():
    place = lax.broadcasted_iota(jnp.int32, (8, C), 0)
    return (place < 2) | (place >= 6)


def packed(rows):
    own = rows[:, 0:BW].reshape(2 * BW, C)
    side = jnp.where(side_places(), rows[0, BW:CP], pltpu.roll(rows[1, BW:CP], 4, axis=0))
    return jnp.concatenate([own, side], axis=0)


def unpacked(block):
    own, side = block[0 : 2 * BW].reshape(2, BW, C), block[2 * BW :]
    sides = [jnp.where(side_places(), x, 0.0) for x in (side, pltpu.roll(side, 4, axis=0))]
    return jnp.concatenate([own, jnp.stack(sides, 0)], axis=1)


def from_rows(where, one, two):
    below = where["first_below"]
    return jnp.where(below, two, one), jnp.where(below, one, two)


def up_taps(up, upw):
    rows = (((1, 2), (0,)), ((0, 1), (2,)))
    columns = ((1, 2), (0, 1), (0,), (2,))
    for k in range(2):
        for a in range(2):
            sums = [sum(up[dr, dc].astype(F32) for dr in rows[k][a]) for dc in range(3)]
            for b in range(4):
                total = sum(sums[dc] for dc in columns[b])
                upw[k, b * (C // 2) : (b + 1) * (C // 2), a * C : (a + 1) * C] = total.astype(BF)


def grad_hidden_kernel(sizes, counts, pg, rim_one, rim_two, up, own, out, upw, parts, acc):
    where = place_of(sizes)
    up_taps(up, upw)
    length = counts[where["section"]]
    mask = column_mask(where, C, 2)
    low = lax.broadcasted_iota(jnp.int32, (1, CP, C), 2) < C // 2
    for f in range(F):
        side = side_columns(where, rim_one, rim_two, BR * F + f * 2 * BR, 2 * BR)
        for r in range(0, 2 * BR, 2):
            whole = jnp.concatenate([pg[f, r : r + 2].astype(F32), side[r : r + 2]], axis=1)
            whole = jnp.where(mask & (f < length), whole, 0.0)
            mix = jnp.where(low, shifted(whole, 1), shifted(whole, -1))
            for k in range(2):
                rows = slice((r // 2) * CP, (r // 2 + 1) * CP)
                parts[k, f, rows, 0:C] = whole[k].astype(BF)
                parts[k, f, rows, C : 2 * C] = mix[k].astype(BF)
    even = parts[0].reshape(F * BR * CP, 2 * C)
    odd = parts[1].reshape(F * BR * CP, 2 * C)

    def term(x, k, a):
        taps = upw[k, :, a * C : (a + 1) * C]
        return jnp.dot(x, taps, preferred_element_type=F32).reshape(F, BR * CP, C)

    acc[:, CP : 5 * CP] = term(even, 0, 0) + term(odd, 1, 0)
    acc[:, 0:CP] = jnp.zeros((F, CP, C), F32)
    acc[:, 5 * CP : 6 * CP] = jnp.zeros((F, CP, C), F32)
    acc[:, 0 : 4 * CP] += term(even, 0, 1)
    acc[:, 2 * CP : 6 * CP] += term(odd, 1, 1)
    inner = column_mask(where, C, 1)
    for f in range(F):
        value = acc[f].reshape(6, CP, C)
        row = lax.broadcasted_iota(jnp.int32, (6, CP, C), 0)
        keep = inner & ((row > 0) | where["up"]) & ((row < 5) | where["down"])
        out[f] = jnp.where(keep, value, 0.0).astype(BF)


def back_kernel(gh, weight, acc_out, early_out, cells, acc):
    for f in range(F):
        value = gh[f].astype(F32)
        for dc in range(3):
            moved = value if dc == 1 else shifted(value, 1 - dc)
            cells[f, :, dc * C : (dc + 1) * C] = moved[:, 0:BW].reshape(6 * BW, C).astype(BF)
    acc[...] = jnp.zeros(acc.shape, F32)
    left = cells[...].reshape(F * 6 * BW, 3 * C)
    for dt in (2, 1, 0):
        taps = jnp.concatenate(
            [
                jnp.concatenate([weight[dt, dr, dc] for dc in range(3)], axis=1)
                for dr in range(3)
            ],
            axis=0,
        )
        product = lax.dot_general(left, taps, NT, preferred_element_type=F32)
        for dr in range(3):
            for f in range(F):
                acc[f + dt, dr * BW : (dr + 6) * BW] += product[
                    f * 6 * BW : (f + 1) * 6 * BW, dr * C : (dr + 1) * C
                ]
    early_out[...] = acc[0:2].astype(BF)
    acc_out[...] = acc[2:6]


def edge_frames_kernel(sizes, counts, own, one, two, early, out):
    where = place_of(sizes)
    length = counts[where["section"]]
    for k in range(2):
        f = length - 2 + k
        above, below = from_rows(where, one[f].astype(F32), two[f].astype(F32))
        out[k, 0] = jnp.where(where["up"], above, 0.0).astype(BF)
        for r in range(2):
            out[k, 1 + r] = packed(own[f, 2 * r : 2 * r + 2].astype(F32)).astype(BF)
        out[k, 3] = jnp.where(where["down"], below, 0.0).astype(BF)


def side_by_side(x, rows, cells, f):
    for dc in range(3):
        moved = x if dc == 1 else shifted(x, dc - 1)
        count = x.shape[0] * CP
        cells[f, rows * CP : rows * CP + count, dc * C : (dc + 1) * C] = moved.reshape(
            count, C
        ).astype(BF)


def forward_own_kernel(own, weight, edge, acc, cells):
    for f in range(F):
        side_by_side(own[f].astype(F32), 0, cells, f)
    acc[...] = jnp.zeros(acc.shape, F32)
    for dt in (2, 1, 0):
        count = F - (2 - dt)
        taps = jnp.concatenate([weight[dt, dr] for dr in range(3)], axis=1)
        left = cells[0:count].reshape(count * BR * CP, 3 * C)
        product = jnp.dot(left, taps, preferred_element_type=F32)
        for dr in range(3):
            for f in range(count):
                acc[f + 2 - dt, (2 - dr) * CP : (6 - dr) * CP] += product[
                    f * BR * CP : (f + 1) * BR * CP, dr * C : (dr + 1) * C
                ]


def forward_rim_kernel(sizes, one, two, part, weight, mine, acc, cells):
    where = place_of(sizes)
    for f in range(F):
        above, below = from_rows(where, one[f].astype(F32), two[f].astype(F32))
        side_by_side(jnp.where(where["up"], unpacked(above), 0.0), 0, cells, f)
        side_by_side(jnp.where(where["down"], unpacked(below), 0.0), 2, cells, f)
    acc[...] = part[...]
    for dt in (2, 1, 0):
        count = F - (2 - dt)
        terms = []
        for dr in range(3):
            left = cells[0:count, dr * CP : (dr + 2) * CP].reshape(count * 2 * CP, 3 * C)
            term = jnp.dot(left, weight[dt, dr], preferred_element_type=F32)
            terms.append(term.reshape(count, 2 * CP, C))
        acc[2 - dt : F, 0 : 2 * CP] += terms[0]
        acc[2 - dt : F, 0:CP] += terms[1][:, 0:CP]
        acc[2 - dt : F, 5 * CP : 6 * CP] += terms[1][:, CP : 2 * CP]
        acc[2 - dt : F, 4 * CP : 6 * CP] += terms[2]


def decode_kernel(sizes, counts, part, prior, weight, upw, out_hbm, mark, cells, pairs, out, sems):
    where = place_of(sizes)
    length = counts[where["section"]]
    for k in range(2):
        for r in range(4):
            rows = jnp.where(where["before"], unpacked(prior[k, r].astype(F32)), 0.0)
            side_by_side(rows, 2 * r, cells, k)

    def term(first, count, dt):
        total = None
        for dr in range(3):
            left = cells[first : first + count, dr * CP : (dr + 6) * CP].reshape(count * 6 * CP, 3 * C)
            value = jnp.dot(left, weight[dt, dr], preferred_element_type=F32)
            total = value if total is None else total + value
        return total.reshape(count, 6 * CP, C)

    early = part[0:2] + term(0, 2, 0)
    late = term(1, 1, 1)
    inner = column_mask(where, C, 1)
    row = lax.broadcasted_iota(jnp.int32, (6, CP, C), 0)
    keep = inner & ((row > 0) | where["up"]) & ((row < 5) | where["down"])
    for f in range(F):
        value = part[f] if f >= 2 else early[f]
        if f == 0:
            value = value + late[0]
        hidden = jnp.where(keep, value.reshape(6, CP, C), 0.0).reshape(6 * CP, C).astype(BF)
        pairs[0, f, :, 0:C] = hidden[CP : 5 * CP]
        pairs[0, f, :, C : 2 * C] = hidden[0 : 4 * CP]
        pairs[1, f, :, 0:C] = hidden[CP : 5 * CP]
        pairs[1, f, :, C : 2 * C] = hidden[2 * CP : 6 * CP]
    low = lax.broadcasted_iota(jnp.int32, (1, CP, C), 2) < C // 2
    products = [
        lax.dot_general(
            pairs[k].reshape(F * 4 * CP, 2 * C), upw[k], NT, preferred_element_type=F32
        )
        for k in range(2)
    ]
    copies = []
    for f in range(F):
        for k in range(2):
            whole = products[k][f * 4 * CP : (f + 1) * 4 * CP].reshape(4, CP, 2 * C)
            side = whole[:, :, C : 2 * C]
            mix = jnp.where(low, shifted(side, -1), shifted(side, 1))
            value = jnp.where(f < length, whole[:, :, 0:C] + mix, 0.0)[:, 0:BW].astype(BF)
            for r in range(BR):
                out[f, 2 * r + k] = value[r]
        copies.append(pltpu.make_async_copy(out.at[f], out_hbm.at[f], sems.at[f]))
        copies[f].start()
    mark[...] = jnp.zeros(mark.shape, F32)
    for copy in copies:
        copy.wait()


def later_group_kernel(sizes, counts, acc, later, one, two, own):
    where = place_of(sizes)
    length = jnp.where(where["after"], counts[where["section"]], -8)
    below = where["first_below"]
    for f in range(F):
        total = acc[f]
        for k in range(2):
            total = total + jnp.where(f == length - 2 + k, later[k].astype(F32), 0.0)
        top, bottom = total[0 : 2 * BW], total[6 * BW : 8 * BW]
        one[f] = jnp.where(below, bottom, top).astype(BF)
        two[f] = jnp.where(below, top, bottom).astype(BF)
        own[f] = total[2 * BW : 6 * BW]


def latent_grad_kernel(sizes, counts, lat, gain, own, one, two, mark, out_hbm, out, sems):
    where = place_of(sizes)
    length = counts[where["section"]]
    g = gain[...].reshape(1, 1, C)
    copies = []
    for f in range(F):
        x = lat[f].astype(F32)
        above, below = from_rows(where, one[f].astype(F32), two[f].astype(F32))
        upper = own[f, 0 : 2 * BW] + jnp.where(where["up"], above, 0.0)
        lower = own[f, 2 * BW : 4 * BW] + jnp.where(where["down"], below, 0.0)
        grad = jnp.concatenate([upper, lower], 0).reshape(BR, BW, C)
        scale = lax.rsqrt(jnp.mean(x * x, axis=-1, keepdims=True) + EPS)
        unit = x * scale
        v = unit * g
        s = jax.nn.sigmoid(v)
        t = grad * (s + v * s * (1.0 - s)) * g
        slope = jnp.mean(t * unit, axis=-1, keepdims=True)
        out[f] = jnp.where(f < length, scale * (t - unit * slope), 0.0)
        copies.append(pltpu.make_async_copy(out.at[f], out_hbm.at[f], sems.at[f]))
        copies[f].start()
    for copy in copies:
        copy.wait()


def call(kernel, outs, ins, scratch=(), flops=0, limit=40, outs_at=None, aliases=None):
    return pl.pallas_call(
        kernel,
        out_shape=outs,
        in_specs=ins,
        out_specs=outs_at or jax.tree.map(lambda _: VM, outs),
        scratch_shapes=list(scratch),
        input_output_aliases=aliases or {},
        compiler_params=pltpu.CompilerParams(vmem_limit_bytes=limit * 2**20),
        cost_estimate=pl.CostEstimate(flops=flops, bytes_accessed=1000000, transcendentals=0),
    )


def ring(value, axis, steps):
    count = lax.axis_size(axis)
    return lax.ppermute(value, axis, [(i, (i + steps) % count) for i in range(count)])


def swap(value, tiles, unit, second):
    shift = GCOL + 1 + second * unit
    return lax.ppermute(
        value, "tile", [(at, (((at + shift) ^ unit) - shift) % tiles) for at in range(tiles)]
    )


def per_device(latents, counts, norm_gain, conv_weight, up_weight, pixel_grad):
    sizes = (lax.axis_size("section"), lax.axis_size("tile"))
    lat, pg = latents[:, 0], pixel_grad[:, 0]
    gain = norm_gain.reshape(1, C)
    sd = jax.ShapeDtypeStruct
    kern = lambda k: functools.partial(k, sizes)
    wide = conv_weight.reshape(3, 3, 3 * C, C)

    tiles = sizes[1]
    side = sd((2, 3 * BR * F, C), BF)
    side_one, side_two = call(kern(strips_kernel), (side, side), [VM, VM], flops=4 * 10**9)(lat, pg)
    side_one, side_two = swap(side_one, tiles, 1, 0), swap(side_two, tiles, 1, 1)
    rim = sd((F, 2 * BW + 8, C), BF)
    own, one, two = call(
        kern(acts_kernel), (sd((F, BR, CP, C), BF), rim, rim), [VM, VM, VM, VM], flops=4 * 10**9
    )(lat, side_one, side_two, gain)
    one, two = swap(one, tiles, GCOL, 0), swap(two, tiles, GCOL, 1)
    gh, upw = call(
        kern(grad_hidden_kernel),
        (sd((F, 6, CP, C), BF), sd((2, 2 * C, 2 * C), BF)),
        [SM, VM, VM, VM, VM, ANY],
        [pltpu.VMEM((2, F, BR * CP, 2 * C), BF), pltpu.VMEM((F, 6 * CP, C), F32)],
        flops=3 * 10**9,
    )(counts, pg, side_one, side_two, jnp.transpose(up_weight, (0, 1, 3, 2)), own)
    acc, early = call(
        back_kernel,
        (sd((F, 8 * BW, C), F32), sd((2, 8 * BW, C), BF)),
        [VM, VM],
        [
            pltpu.VMEM((F, 6 * BW, 3 * C), BF),
            pltpu.VMEM((F + 2, 8 * BW, C), F32),
        ],
        flops=6 * 10**9,
    )(gh, conv_weight)
    edge = call(
        kern(edge_frames_kernel), sd((2, 4, 2 * BW + 8, C), BF), [SM, VM, VM, VM, ANY]
    )(counts, own, one, two, early)
    prior = ring(edge, "section", 1)
    later = ring(early, "section", -1)
    partial = sd((F, 6 * CP, C), F32)
    part = call(
        forward_own_kernel,
        partial,
        [VM, VM, ANY],
        [pltpu.VMEM((F, BR * CP, 3 * C), BF)],
        flops=4 * 10**9,
    )(own, wide, edge)
    rims = one, two
    one, two, mine = call(
        kern(later_group_kernel),
        (sd((F, 2 * BW, C), BF), sd((F, 2 * BW, C), BF), sd((F, 4 * BW, C), F32)),
        [SM, VM, VM],
    )(counts, acc, later)
    one, two = swap(one, tiles, GCOL, 0), swap(two, tiles, GCOL, 1)
    part = call(
        kern(forward_rim_kernel),
        partial,
        [VM, VM, VM, VM, ANY],
        [pltpu.VMEM((F, BR * CP, 3 * C), BF)],
        flops=3 * 10**9,
    )(*rims, part, wide, mine)
    decoded, mark = call(
        kern(decode_kernel),
        (sd((F, 2 * BR, BW, C), BF), sd((8, 128), F32)),
        [SM, VM, VM, VM, VM],
        [
            pltpu.VMEM((2, 8 * CP, 3 * C), BF),
            pltpu.VMEM((2, F, 4 * CP, 2 * C), BF),
            pltpu.VMEM((F, 2 * BR, BW, C), BF),
            pltpu.SemaphoreType.DMA((F,)),
        ],
        outs_at=(ANY, VM),
        flops=4 * 10**9,
    )(counts, part, prior, wide, upw)
    grad = call(
        kern(latent_grad_kernel), sd((F, BR, BW, C), F32), [SM, VM, VM, VM, VM, VM, ANY],
        [pltpu.VMEM((F, BR, BW, C), F32), pltpu.SemaphoreType.DMA((F,))],
        outs_at=ANY,
    )(counts, lat, gain, mine, one, two, mark)
    return (decoded[:, None], grad[:, None])


def solution(mesh):
    blocks = P("section", "tile", None, None, None)
    return jax.shard_map(
        per_device,
        mesh=mesh,
        in_specs=(blocks, P(), P(), P(), P(), blocks),
        out_specs=(blocks, blocks),
        check_vma=False,
    )
```
